128 devices in a mesh: comp: 2 (over z_hi), face: 4 (over z_lo, core), tile: 16 (over y, x).
Axes of the slice: x: 4, y: 4, z: 4 (z_hi: 2, z_lo: 2; z = z_hi * 2 + z_lo), core: 2. Of those that a mesh axis runs over, the one named last changes fastest.
Arguments:
- state: bfloat16 [2, 393216, 256], P('comp', ('face', 'tile')), may hold values from -6 to 6
- cycle_source: int32 [2, 22784], P('comp', ('face', 'tile')), may hold values from 0 to 4095
- halo_rows: int32 [2, 4, 65536], P('comp', None, ('face', 'tile')), may hold values from 0 to 6143
- halo_count: int32 [2, 4, 64], P('comp', None, ('face', 'tile')), may hold values from 256 to 1024, as said below
- couple_rows: int32 [2, 16, 8192], P('comp', None, ('face', 'tile')), may hold values from 0 to 6143, as said below
- couple_count: int32 [2, 16, 64], P('comp', None, ('face', 'tile')), may hold values from 32 to 128, as said below
- couple_land: int32 [2, 16, 8192], P('comp', None, ('face', 'tile')), may hold values from 0 to 6143, as said below
- couple_weight: bfloat16 [2, 256, 256], P('comp'), may hold values from -0.375 to 0.375
- dw_weight: float32 [2, 9, 256], P('comp'), may hold values from -2 to 2
- norm_gain: float32 [2, 256], P('comp'), may hold values from 0.25 to 1.75
- up_weight: bfloat16 [2, 256, 1024], P('comp'), may hold values from -0.375 to 0.375
- up_bias: float32 [2, 1024], P('comp'), may hold values from -3 to 3
- down_weight: bfloat16 [2, 1024, 256], P('comp'), may hold values from -0.1875 to 0.1875
Outputs:
- level_out: bfloat16 [2, 393216, 256], P('comp', ('face', 'tile'))
The draws below stay inside these ranges and needn't reach their ends.
Inputs may be any that keep to these rules, and one draw needn't show every extreme that they name: `halo_count`: in each component and each direction some block sends exactly 1024 rows. `couple_count`: in every draw some block receives 128 rows from each of the 16 blocks of the other component in its face group. `couple_rows`: within one block the 2048 entries are distinct. `couple_land`: within one receiving block the 2048 entries are distinct.
All inputs are finite; a program needn't handle non-finite values.
Results may differ from the reference program's by a relative error of at most 0.0046.
Values may be sent and summed in bfloat16 or wider, within the bound.
A program may use at most 64 MiB of HBM per device.

```python
import jax
import jax.numpy as jnp
from jax import lax

CHANNELS = 256
MLP_WIDTH = 1024
KERNEL_TAPS = 9
GRID_W = 128
CELL_DEV = 6144
HALO_ROWS = 1024
PAIR_SLOTS = 128
CYCLE = 356
BLOCKS = 64
ALL_CELLS = 393216
N_FACE = 4
N_TILE = 16


def distinct_rows(key):
    keys = jax.random.split(key, 2 * BLOCKS)
    chosen = jax.vmap(lambda single: jax.random.permutation(single, CELL_DEV)[:N_TILE * PAIR_SLOTS])(keys)
    chosen = chosen.reshape(2, BLOCKS, N_TILE, PAIR_SLOTS).transpose(0, 2, 1, 3)
    return chosen.reshape(2, N_TILE, BLOCKS * PAIR_SLOTS).astype(jnp.int32)


def draw_couple_rows(key, part):
    key = jax.random.fold_in(key, 11)
    return distinct_rows(key)


def draw_couple_land(key, part):
    key = jax.random.fold_in(key, 13)
    return distinct_rows(key)


def draw_couple_count(key, part):
    key = jax.random.fold_in(key, 17)
    first, second = jax.random.split(key)
    base = jax.random.randint(first, (2, N_TILE, BLOCKS), PAIR_SLOTS // 4, PAIR_SLOTS + 1, dtype=jnp.int32)
    picks = jax.random.randint(second, (3,), 0, 1 << 20, dtype=jnp.int32)
    receiver = picks[0] % 2
    face_pick = picks[1] % N_FACE
    tile_pick = picks[2] % N_TILE
    comp_iota = lax.broadcasted_iota(jnp.int32, (2, N_TILE, BLOCKS), 0)
    dest_iota = lax.broadcasted_iota(jnp.int32, (2, N_TILE, BLOCKS), 1)
    block_iota = lax.broadcasted_iota(jnp.int32, (2, N_TILE, BLOCKS), 2)
    full = (comp_iota == 1 - receiver) & (dest_iota == tile_pick) & (block_iota // N_TILE == face_pick)
    return jnp.where(full, PAIR_SLOTS, base).astype(jnp.int32)


def draw_halo_count(key, part):
    key = jax.random.fold_in(key, 19)
    first, second = jax.random.split(key)
    base = jax.random.randint(first, (2, 4, BLOCKS), HALO_ROWS // 4, HALO_ROWS + 1, dtype=jnp.int32)
    chosen = jax.random.randint(second, (2, 4, 1), 0, BLOCKS, dtype=jnp.int32)
    block_iota = lax.broadcasted_iota(jnp.int32, (2, 4, BLOCKS), 2)
    return jnp.where(block_iota == chosen, HALO_ROWS, base).astype(jnp.int32)


def with_ends(result, own_key, smallest, high):
    shape = result.shape
    place = [jax.random.randint(jax.random.fold_in(own_key, axis), (), 0, shape[axis]) for axis in range(len(shape))]
    result = result.at[tuple(place)].set(smallest)
    longest = shape.index(max(shape))
    place[longest] = (place[longest] + 1) % shape[longest]
    return result.at[tuple(place)].set(high)


def level_of(own_key, shape, pieces, smallest, high):
    factor_of, own = 1.0, jax.random.fold_in(own_key, 6)
    for position, blocks in pieces:
        draws = jnp.exp(jax.random.uniform(jax.random.fold_in(own, position), (blocks,), jnp.float32, smallest / len(pieces), high / len(pieces)))
        factor_of = factor_of * jnp.repeat(draws, shape[position] // blocks).reshape([-1 if axis == position else 1 for axis in range(len(shape))])
    return factor_of


def gaussian(key, shape, deviation, most, cuts=(), held_as=jnp.bfloat16):
    level = level_of(key, shape, cuts, -0.22, 0.18) if cuts else 1.0
    result = jax.random.normal(key, shape, jnp.float32) * deviation * level
    return jnp.minimum(jnp.maximum(result, -most), most).astype(held_as)


def setup_inputs(seed: int = 0) -> dict:
    key_of = jax.random.split(jax.random.key(seed), 14)
    state = gaussian(key_of[0], (2, ALL_CELLS, CHANNELS), 1.0, 6.0, ((0, 2), (1, 64)))
    cycle_source = with_ends(jax.random.randint(key_of[1], (2, BLOCKS * CYCLE), 0, 4 * HALO_ROWS), jax.random.fold_in(key_of[1], 1), 0, (4 * HALO_ROWS) - 1).astype(jnp.int32)
    halo_rows = with_ends(jax.random.randint(key_of[2], (2, 4, BLOCKS * HALO_ROWS), 0, CELL_DEV), jax.random.fold_in(key_of[2], 1), 0, CELL_DEV - 1).astype(jnp.int32)
    halo_count = draw_halo_count(jax.random.fold_in(key_of[13], 71), 0)
    couple_rows = draw_couple_rows(jax.random.fold_in(key_of[13], 71), 0)
    couple_count = draw_couple_count(jax.random.fold_in(key_of[13], 71), 0)
    couple_land = draw_couple_land(jax.random.fold_in(key_of[13], 71), 0)
    couple_weight = gaussian(key_of[7], (2, CHANNELS, CHANNELS), CHANNELS ** -0.5, 0.375, ((0, 2),))
    dw_weight = gaussian(key_of[8], (2, KERNEL_TAPS, CHANNELS), KERNEL_TAPS ** -0.5, 2.0, ((0, 2),), jnp.float32)
    norm_gain = jnp.clip(1.0 + 0.15 * jax.random.normal(key_of[9], (2, CHANNELS), jnp.float32), 0.25, 1.75)
    up_weight = gaussian(key_of[10], (2, CHANNELS, MLP_WIDTH), CHANNELS ** -0.5, 0.375, ((0, 2),))
    up_bias = gaussian(key_of[11], (2, MLP_WIDTH), 0.5, 3.0, ((0, 2),), jnp.float32)
    down_weight = gaussian(key_of[12], (2, MLP_WIDTH, CHANNELS), MLP_WIDTH ** -0.5, 0.1875, ((0, 2),))
    return dict(state=state, cycle_source=cycle_source, halo_rows=halo_rows, halo_count=halo_count, couple_rows=couple_rows, couple_count=couple_count, couple_land=couple_land, couple_weight=couple_weight, dw_weight=dw_weight, norm_gain=norm_gain, up_weight=up_weight, up_bias=up_bias, down_weight=down_weight)


def pick_rows(rows, index):
    return rows[index]

def padded_grid(joined_rows, rim_rows, cycle_index):
    height = joined_rows.shape[0] // GRID_W
    channels = joined_rows.shape[1]
    grid = joined_rows.reshape(height, GRID_W, channels)
    border = rim_rows[cycle_index]
    top = border[:GRID_W + 2]
    bottom = border[GRID_W + 2:2 * GRID_W + 4]
    left = border[2 * GRID_W + 4:2 * GRID_W + 4 + height]
    right = border[2 * GRID_W + 4 + height:]
    middle = jnp.concatenate([left[:, None], grid, right[:, None]], 1)
    return jnp.concatenate([top[None], middle, bottom[None]], 0)

def depthwise(padded, dw_taps, height):
    channels = padded.shape[2]
    mixed = jnp.zeros((height, GRID_W, channels), jnp.float32)
    for row_step in range(3):
        for col_step in range(3):
            window = padded[row_step:row_step + height, col_step:col_step + GRID_W]
            mixed = mixed + dw_taps[3 * row_step + col_step] * window.astype(jnp.float32)
    return mixed.reshape(height * GRID_W, channels)

def level_block(joined_rows, rim_rows, cycle_index, dw_taps, gain, w_up, b_up, w_down):
    height = joined_rows.shape[0] // GRID_W
    padded = padded_grid(joined_rows, rim_rows, cycle_index)
    mixed = depthwise(padded, dw_taps, height)
    center = mixed - lax.optimization_barrier(jnp.mean(mixed, axis=-1, keepdims=True))
    spread = lax.optimization_barrier(jnp.mean(center * center, axis=-1, keepdims=True))
    normed = (center * lax.rsqrt(spread + 1e-06) * gain).astype(jnp.bfloat16)
    before = jnp.dot(normed, w_up, preferred_element_type=jnp.float32) + b_up
    hidden = jax.nn.gelu(before, approximate=True).astype(jnp.bfloat16)
    output = joined_rows.astype(jnp.float32) + jnp.dot(hidden, w_down, preferred_element_type=jnp.float32)
    return output.astype(jnp.bfloat16)

def reference(state, cycle_source, halo_rows, halo_count, couple_rows, couple_count, couple_land, couple_weight, dw_weight, norm_gain, up_weight, up_bias, down_weight):
    blocks = state.reshape(2, N_FACE, N_TILE, CELL_DEV, CHANNELS)
    send_index = couple_rows.reshape(2, N_TILE, N_FACE, N_TILE, PAIR_SLOTS).transpose(0, 2, 3, 1, 4)
    send_index = send_index.reshape(2, N_FACE, N_TILE, N_TILE * PAIR_SLOTS)
    picked = jax.vmap(jax.vmap(jax.vmap(pick_rows)))(blocks, send_index)
    picked = picked.reshape(2, N_FACE, N_TILE, N_TILE, PAIR_SLOTS, CHANNELS)
    counts = couple_count.reshape(2, N_TILE, N_FACE, N_TILE).transpose(0, 2, 3, 1)
    slot_iota = jnp.arange(PAIR_SLOTS, dtype=jnp.int32)
    live = slot_iota[None, None, None, None, :] < counts[..., None]
    sent = jnp.where(live[..., None], picked, jnp.zeros((), jnp.bfloat16))
    received = sent[::-1].transpose(0, 1, 3, 2, 4, 5).reshape(2, N_FACE, N_TILE, N_TILE * PAIR_SLOTS, CHANNELS)
    projected = jnp.einsum('cfjnd,cde->cfjne', received.astype(jnp.float32), couple_weight.astype(jnp.float32))
    landing = couple_land.reshape(2, N_TILE, N_FACE, N_TILE, PAIR_SLOTS).transpose(0, 2, 3, 1, 4)
    landing = landing.reshape(2 * BLOCKS, N_TILE * PAIR_SLOTS)

    def land_rows(inputs):
        rows, where_to, values = inputs
        added = jnp.zeros((CELL_DEV, CHANNELS), jnp.float32).at[where_to].add(values)
        return (rows.astype(jnp.float32) + added).astype(jnp.bfloat16)
    joined = lax.map(land_rows, (state.reshape(2 * BLOCKS, CELL_DEV, CHANNELS), landing, projected.reshape(2 * BLOCKS, N_TILE * PAIR_SLOTS, CHANNELS)))
    rim_index = halo_rows.reshape(2, 4, BLOCKS, HALO_ROWS).transpose(0, 2, 1, 3).reshape(2 * BLOCKS, 4 * HALO_ROWS)
    rim_pick = jax.vmap(pick_rows)(joined, rim_index).reshape(2, N_FACE, N_TILE, 4, HALO_ROWS, CHANNELS)
    rim_count = halo_count.transpose(0, 2, 1).reshape(2, N_FACE, N_TILE, 4)
    rim_live = jnp.arange(HALO_ROWS, dtype=jnp.int32)[None, None, None, None, :] < rim_count[..., None]
    packs = jnp.where(rim_live[..., None], rim_pick, jnp.zeros((), jnp.bfloat16))
    from_lower_tile = jnp.roll(packs[:, :, :, 0], 1, axis=2)
    from_upper_tile = jnp.roll(packs[:, :, :, 1], -1, axis=2)
    from_lower_face = jnp.roll(packs[:, :, :, 2], 1, axis=1)
    from_upper_face = jnp.roll(packs[:, :, :, 3], -1, axis=1)
    rims = jnp.stack([from_lower_tile, from_upper_tile, from_lower_face, from_upper_face], axis=3)
    rims = rims.reshape(2, BLOCKS, 4 * HALO_ROWS, CHANNELS)
    joined = joined.reshape(2, BLOCKS, CELL_DEV, CHANNELS)
    cycle_blocks = cycle_source.reshape(2, BLOCKS, CYCLE)
    results = []
    for component in range(2):

        def one_block(inputs, component=component):
            return level_block(inputs[0], inputs[1], inputs[2], dw_weight[component], norm_gain[component], up_weight[component], up_bias[component], down_weight[component])
        results.append(lax.map(one_block, (joined[component], rims[component], cycle_blocks[component])))
    return jnp.stack(results, 0).reshape(2, ALL_CELLS, CHANNELS)
```

```python
import functools

import jax
import jax.numpy as jnp
from jax import lax
from jax.experimental import pallas as pl
from jax.experimental.pallas import tpu as pltpu
from jax.sharding import PartitionSpec as P

MESH = pl.DeviceIdType.MESH
GRID_W = 128
F32 = jnp.float32
BF16 = jnp.bfloat16


def place(comp, face, tile):
    return {"comp": comp, "face": face, "tile": tile}


def couple_kernel(
    tiles,
    faces,
    cycle_len,
    border_rows,
    state_ref,
    cycle_ref,
    halo_rows_ref,
    halo_count_ref,
    couple_rows_ref,
    couple_count_ref,
    couple_land_ref,
    couple_weight_ref,
    dw_ref,
    gain_ref,
    joined_out,
    normed_out,
    rows_bf,
    rows_f32,
    picked,
    send_rows,
    recv_rows,
    cycle_near,
    cycle_smem,
    halo_index,
    halo_send,
    halo_recv,
    border,
    columns,
    edge,
    normed,
    load_sem,
    smem_sem,
    store_sem,
    couple_send_sem,
    couple_recv_sem,
    cycle_send_sem,
    cycle_recv_sem,
    halo_send_sem,
    halo_recv_sem,
):
    comp, face, tile = lax.axis_index("comp"), lax.axis_index("face"), lax.axis_index("tile")
    cells, channels = rows_bf.shape
    height = cells // GRID_W
    slots = couple_rows_ref.shape[2]
    rim_rows = halo_rows_ref.shape[2]
    other = 1 - comp
    near = [
        place(comp, face, lax.rem(tile + 1, tiles)),
        place(comp, face, lax.rem(tile + tiles - 1, tiles)),
        place(comp, lax.rem(face + 1, faces), tile),
        place(comp, lax.rem(face + faces - 1, faces), tile),
    ]

    load_chunks = 4
    chunk = cells // load_chunks

    def load(k):
        part = pl.ds(k * chunk, chunk)
        return pltpu.make_async_copy(state_ref.at[0, part], rows_bf.at[part], load_sem.at[k])

    for k in range(load_chunks):
        load(k).start()

    barrier = pltpu.get_barrier_semaphore()

    def greet(k, carry):
        pl.semaphore_signal(barrier, inc=1, device_id=place(other, face, k), device_id_type=MESH)
        return carry

    lax.fori_loop(0, tiles, greet, 0)
    for target in near:
        pl.semaphore_signal(barrier, inc=1, device_id=target, device_id_type=MESH)

    rows_f32[pl.ds(cells, 8), :] = jnp.zeros((8, channels), F32)
    for k in range(load_chunks):
        load(k).wait()

        def widen(i, carry, k=k):
            part = pl.ds(pl.multiple_of(k * chunk + i * 128, 128), 128)
            rows_f32[part, :] = rows_bf[part, :].astype(F32)
            return carry

        lax.fori_loop(0, chunk // 128, widen, 0)

    pl.semaphore_wait(barrier, tiles + 4)

    def cycle_copy(d):
        return pltpu.make_async_remote_copy(
            src_ref=cycle_ref,
            dst_ref=cycle_near.at[d],
            send_sem=cycle_send_sem.at[d],
            recv_sem=cycle_recv_sem.at[d],
            device_id=near[d ^ 1],
            device_id_type=MESH,
        )

    for d in range(4):
        cycle_copy(d).start()

    def couple_copy(k):
        part = pl.ds(pl.multiple_of(k * slots, slots), slots)
        return pltpu.make_async_remote_copy(
            src_ref=send_rows.at[part],
            dst_ref=recv_rows.at[part],
            send_sem=couple_send_sem.at[k],
            recv_sem=couple_recv_sem.at[k],
            device_id=place(other, face, lax.rem(tile + k, tiles)),
            device_id_type=MESH,
        )

    def gather_send(k, carry):
        dest = lax.rem(tile + k, tiles)
        live = couple_count_ref[0, dest, 0]

        def pick(g, inner):
            for u in range(8):
                s = g * 8 + u
                index = jnp.where(s < live, couple_rows_ref[0, dest, s], cells)
                picked[pl.ds(s, 1), :] = rows_f32[pl.ds(index, 1), :]
            return inner

        lax.fori_loop(0, slots // 8, pick, 0)
        part = pl.ds(pl.multiple_of(k * slots, slots), slots)
        send_rows[part, :] = picked[pl.ds(0, slots), :].astype(BF16)
        couple_copy(k).start()
        return carry

    lax.fori_loop(0, tiles, gather_send, 0)

    for d in range(4):
        cycle_copy(d).wait()
    to_smem = pltpu.make_async_copy(cycle_near, cycle_smem, smem_sem)
    to_smem.start()
    to_smem.wait()
    for d in range(4):
        live = halo_count_ref[0, d, 0]

        def resolve(g, carry, d=d, live=live):
            for u in range(4):
                r = g * 4 + u
                asked = cycle_smem[d, 0, r]
                s = jnp.bitwise_and(asked, rim_rows - 1)
                mine = (asked >= d * rim_rows) & (asked < (d + 1) * rim_rows) & (s < live)
                halo_index[d, r] = jnp.where(mine, halo_rows_ref[0, d, s], cells)
            return carry

        lax.fori_loop(0, cycle_len // 4, resolve, 0)

        def unasked(r, carry, d=d):
            halo_index[d, r] = cells
            return carry

        lax.fori_loop(cycle_len, border_rows, unasked, 0)

    pair = 2 * slots
    span = 4
    lane_col = lax.broadcasted_iota(jnp.int32, (GRID_W, pair), 0)

    def land_pair(p, last):
        part = pl.ds(pl.multiple_of(p * pair, pair), pair)
        rows = recv_rows[part, :]
        arrived = jnp.dot(rows, couple_weight_ref[0], preferred_element_type=F32)
        high = arrived.astype(BF16)
        low = (arrived - high.astype(F32)).astype(BF16)
        land = jnp.concatenate(
            [
                couple_land_ref[0, pl.ds(lax.rem(tile - (2 * p + q) + tiles, tiles), 1), :]
                for q in range(2)
            ],
            axis=1,
        )
        land_row = jnp.right_shift(land, 7)
        in_col = jnp.where(jnp.bitwise_and(land, GRID_W - 1) == lane_col, 1.0, 0.0).astype(BF16)

        def block(b, carry):
            hot = jnp.concatenate(
                [
                    in_col * jnp.where(land_row == b * span + q, 1.0, 0.0).astype(BF16)
                    for q in range(span)
                ],
                axis=0,
            )
            where = pl.ds(pl.multiple_of(b * span * GRID_W, span * GRID_W), span * GRID_W)
            added = jnp.dot(hot, high, preferred_element_type=F32)
            added = added + jnp.dot(hot, low, preferred_element_type=F32)
            total = rows_f32[where, :] + added
            if last:
                rounded = total.astype(BF16)
                rows_bf[where, :] = rounded
                total = rounded.astype(F32)
            rows_f32[where, :] = total
            return carry

        lax.fori_loop(0, height // span, block, 0)

    def land_step(p, carry):
        couple_copy(2 * p).wait_recv()
        couple_copy(2 * p + 1).wait_recv()
        land_pair(p, False)
        return carry

    lax.fori_loop(0, tiles // 2 - 1, land_step, 0)
    couple_copy(tiles - 2).wait_recv()
    couple_copy(tiles - 1).wait_recv()
    land_pair(tiles // 2 - 1, True)

    joined_store = pltpu.make_async_copy(rows_bf, joined_out, store_sem.at[0])
    joined_store.start()

    def halo_copy(d):
        return pltpu.make_async_remote_copy(
            src_ref=halo_send.at[d],
            dst_ref=halo_recv.at[d],
            send_sem=halo_send_sem.at[d],
            recv_sem=halo_recv_sem.at[d],
            device_id=near[d],
            device_id_type=MESH,
        )

    for d in (2, 3, 0, 1):

        def pick_halo(g, carry, d=d):
            for u in range(8):
                r = g * 8 + u
                picked[pl.ds(r, 1), :] = rows_f32[pl.ds(halo_index[d, r], 1), :]
            return carry

        lax.fori_loop(0, border_rows // 8, pick_halo, 0)
        halo_send[d] = picked[...].astype(BF16)
        halo_copy(d).start()

    taps = dw_ref[0]
    gain = gain_ref[0:1, :]

    def norm(mixed):
        center = mixed - jnp.mean(mixed, axis=-1, keepdims=True)
        spread = jnp.mean(center * center, axis=-1, keepdims=True)
        return center * lax.rsqrt(spread + 1e-06) * gain

    def mix(above, here, below):
        left, mid, right = (
            taps[c : c + 1] * above + taps[3 + c : 4 + c] * here + taps[6 + c : 7 + c] * below
            for c in range(3)
        )
        return mid + pltpu.roll(left, 1, 0) + pltpu.roll(right, GRID_W - 1, 0)

    def grid_row(i):
        return rows_f32[pl.ds(pl.multiple_of(i * GRID_W, GRID_W), GRID_W), :]

    def interior(i, carry):
        mixed = mix(grid_row(i - 1), grid_row(i), grid_row(i + 1))
        normed[pl.ds(pl.multiple_of(i * GRID_W, GRID_W), GRID_W), :] = norm(mixed).astype(BF16)
        return carry

    lax.fori_loop(1, height - 1, interior, 0)

    for d in range(4):
        halo_copy(d).wait_recv()
    border[...] = (halo_recv[0].astype(F32) + halo_recv[1].astype(F32)) + (
        halo_recv[2].astype(F32) + halo_recv[3].astype(F32)
    )
    wide = GRID_W + 2
    normed[pl.ds(0, GRID_W), :] = norm(
        mix(border[pl.ds(1, GRID_W), :], grid_row(0), grid_row(1))
    ).astype(BF16)
    normed[pl.ds(cells - GRID_W, GRID_W), :] = norm(
        mix(grid_row(height - 2), grid_row(height - 1), border[pl.ds(wide + 1, GRID_W), :])
    ).astype(BF16)

    outer = ((1, 0), (2, 1), (3, GRID_W - 2), (4, GRID_W - 1))

    def take_columns(i, carry):
        for q, col in outer:
            columns[q, pl.ds(i + 1, 1), :] = rows_f32[pl.ds(i * GRID_W + col, 1), :]
        return carry

    lax.fori_loop(0, height, take_columns, 0)
    for q, col in outer:
        columns[q, pl.ds(0, 1), :] = border[pl.ds(1 + col, 1), :]
        columns[q, pl.ds(height + 1, 1), :] = border[pl.ds(wide + 1 + col, 1), :]
    for q, corner, side in ((0, 0, 2 * wide), (5, wide - 1, 2 * wide + height)):
        columns[q, pl.ds(0, 1), :] = border[pl.ds(corner, 1), :]
        columns[q, pl.ds(1, height), :] = border[pl.ds(side, height), :]
        columns[q, pl.ds(height + 1, 1), :] = border[pl.ds(wide + corner, 1), :]
    for e, first in ((0, 0), (1, 3)):
        mixed = jnp.zeros((height, channels), F32)
        for r in range(3):
            for c in range(3):
                mixed = mixed + taps[3 * r + c : 3 * r + c + 1] * columns[first + c, pl.ds(r, height), :]
        edge[e] = norm(mixed)
    tile_rows = 16
    tile_iota = lax.broadcasted_iota(jnp.int32, (tile_rows, channels), 0)

    def merge(i, carry):
        for e, start, line in ((0, 0, 0), (1, GRID_W - tile_rows, tile_rows - 1)):
            part = pl.ds(pl.multiple_of(i * GRID_W + start, tile_rows), tile_rows)
            fixed = jnp.where(tile_iota == line, edge[e, pl.ds(i, 1), :], normed[part, :].astype(F32))
            normed[part, :] = fixed.astype(BF16)
        return carry

    lax.fori_loop(0, height, merge, 0)
    normed_store = pltpu.make_async_copy(normed, normed_out, store_sem.at[1])
    normed_store.start()
    for k in range(tiles):
        couple_copy(k).wait_send()
    for d in range(4):
        halo_copy(d).wait_send()
    joined_store.wait()
    normed_store.wait()


def mlp_kernel(normed_ref, joined_ref, up_ref, bias_ref, down_ref, out_ref):
    normed = normed_ref[...]
    width = up_ref.shape[2]
    total = joined_ref[...].astype(F32)
    step = 256
    for h in range(0, width, step):
        v = jnp.dot(normed, up_ref[0, :, h : h + step], preferred_element_type=F32)
        v = v + bias_ref[0:1, h : h + step]
        inner = v * (0.7978845608028654 + 0.035677408136300125 * (v * v))
        half = 0.5 * v
        hidden = (half + half * jnp.tanh(inner)).astype(BF16)
        total = total + jnp.dot(hidden, down_ref[0, h : h + step, :], preferred_element_type=F32)
    out_ref[0] = total.astype(BF16)


def body(
    state,
    cycle_source,
    halo_rows,
    halo_count,
    couple_rows,
    couple_count,
    couple_land,
    couple_weight,
    dw_weight,
    norm_gain,
    up_weight,
    up_bias,
    down_weight,
):
    _, cells, channels = state.shape
    tiles, faces = lax.axis_size("tile"), lax.axis_size("face")
    cycle_len = cycle_source.shape[1]
    border_rows = -(-cycle_len // 16) * 16
    slots = couple_rows.shape[2]
    height = cells // GRID_W
    vmem = pl.BlockSpec(memory_space=pltpu.VMEM)
    smem = pl.BlockSpec(memory_space=pltpu.SMEM)
    hbm = pl.BlockSpec(memory_space=pl.ANY)
    dma = pltpu.SemaphoreType.DMA
    joined, normed = pl.pallas_call(
        functools.partial(couple_kernel, tiles, faces, cycle_len, border_rows),
        name="couple_and_mix",
        out_shape=[jax.ShapeDtypeStruct((cells, channels), BF16)] * 2,
        in_specs=[hbm, vmem, smem, smem, smem, smem, vmem, vmem, vmem, vmem],
        out_specs=[hbm, hbm],
        scratch_shapes=[
            pltpu.VMEM((cells, channels), BF16),
            pltpu.VMEM((cells + 8, channels), F32),
            pltpu.VMEM((border_rows, channels), F32),
            pltpu.VMEM((tiles * slots, channels), BF16),
            pltpu.VMEM((tiles * slots, channels), BF16),
            pltpu.VMEM((4, 1, cycle_len), jnp.int32),
            pltpu.SMEM((4, 1, cycle_len), jnp.int32),
            pltpu.SMEM((4, border_rows), jnp.int32),
            pltpu.VMEM((4, border_rows, channels), BF16),
            pltpu.VMEM((4, border_rows, channels), BF16),
            pltpu.VMEM((border_rows, channels), F32),
            pltpu.VMEM((6, height + 8, channels), F32),
            pltpu.VMEM((2, height, channels), F32),
            pltpu.VMEM((cells, channels), BF16),
            dma((4,)),
            dma,
            dma((2,)),
            dma((tiles,)),
            dma((tiles,)),
            dma((4,)),
            dma((4,)),
            dma((4,)),
            dma((4,)),
        ],
        compiler_params=pltpu.CompilerParams(
            collective_id=0, has_side_effects=True, vmem_limit_bytes=40 << 20
        ),
    )(
        state,
        cycle_source,
        halo_rows,
        halo_count,
        couple_rows,
        couple_count,
        couple_land,
        couple_weight,
        dw_weight,
        norm_gain,
    )
    rows = 1024
    width = up_weight.shape[2]
    return pl.pallas_call(
        mlp_kernel,
        name="mlp",
        grid=(cells // rows,),
        out_shape=jax.ShapeDtypeStruct((1, cells, channels), BF16),
        in_specs=[
            pl.BlockSpec((rows, channels), lambda i: (i, 0)),
            pl.BlockSpec((rows, channels), lambda i: (i, 0)),
            pl.BlockSpec((1, channels, width), lambda i: (0, 0, 0)),
            pl.BlockSpec((1, width), lambda i: (0, 0)),
            pl.BlockSpec((1, width, channels), lambda i: (0, 0, 0)),
        ],
        out_specs=pl.BlockSpec((1, rows, channels), lambda i: (0, i, 0)),
        compiler_params=pltpu.CompilerParams(vmem_limit_bytes=40 << 20),
        cost_estimate=pl.CostEstimate(
            flops=4 * cells * channels * width, bytes_accessed=6 * cells * channels, transcendentals=cells * width
        ),
    )(normed, joined, up_weight, up_bias, down_weight)


def solution(mesh):
    in_specs = (
        P("comp", ("face", "tile"), None),
        P("comp", ("face", "tile")),
        P("comp", None, ("face", "tile")),
        P("comp", None, ("face", "tile")),
        P("comp", None, ("face", "tile")),
        P("comp", None, ("face", "tile")),
        P("comp", None, ("face", "tile")),
        P("comp", None, None),
        P("comp", None, None),
        P("comp", None),
        P("comp", None, None),
        P("comp", None),
        P("comp", None, None),
    )
    out_specs = P("comp", ("face", "tile"), None)
    return jax.shard_map(body, mesh=mesh, in_specs=in_specs, out_specs=out_specs, check_vma=False)
```

```python
import functools

import jax
import jax.numpy as jnp
from jax import lax
from jax.experimental import pallas as pl
from jax.experimental.pallas import tpu as pltpu
from jax.sharding import PartitionSpec as P

MESH = pl.DeviceIdType.MESH
GRID_W = 128
F32 = jnp.float32
BF16 = jnp.bfloat16
TILE = 16


def place(comp, face, tile):
    return {"comp": comp, "face": face, "tile": tile}


def norm(mixed, gain):
    center = mixed - jnp.mean(mixed, axis=-1, keepdims=True)
    spread = jnp.mean(center * center, axis=-1, keepdims=True)
    return center * lax.rsqrt(spread + 1e-06) * gain


def couple_kernel(
    tiles,
    faces,
    cycle_len,
    state_ref,
    cycle_hbm,
    halo_rows_hbm,
    halo_count_hbm,
    couple_rows_hbm,
    couple_count_hbm,
    couple_land_hbm,
    couple_weight_hbm,
    dw_hbm,
    gain_hbm,
    up_hbm,
    bias_hbm,
    down_hbm,
    out_hbm,
    cycle_ref,
    halo_rows_ref,
    halo_count_ref,
    couple_rows_ref,
    couple_count_ref,
    couple_land_ref,
    couple_weight_ref,
    dw_ref,
    gain_ref,
    up_ref,
    bias_ref,
    down_ref,
    rows_bf,
    rows,
    picked,
    send_rows,
    via_rows,
    recv_rows,
    arrived,
    cycle_near,
    index_i32,
    index_smem,
    index_col,
    halo_part,
    halo_send,
    halo_recv,
    border,
    columns,
    normed,
    out,
    load_sem,
    small_sem,
    smem_sem,
    store_sem,
    cross_send_sem,
    cross_recv_sem,
    pass_send_sem,
    pass_recv_sem,
    cycle_send_sem,
    cycle_recv_sem,
    halo_send_sem,
    halo_recv_sem,
):
    comp, face, tile = lax.axis_index("comp"), lax.axis_index("face"), lax.axis_index("tile")
    cells, channels = rows_bf.shape
    half = channels // 2
    height = cells // GRID_W
    slots = couple_rows_ref.shape[2]
    rim_rows = halo_rows_ref.shape[2]
    border_rows = halo_send.shape[1]
    other = 1 - comp
    near = [
        place(comp, face, lax.rem(tile + 1, tiles)),
        place(comp, face, lax.rem(tile + tiles - 1, tiles)),
        place(comp, lax.rem(face + 1, faces), tile),
        place(comp, lax.rem(face + faces - 1, faces), tile),
    ]

    def get_rows(ref, first, count):
        return jnp.concatenate(
            [ref[pl.ds(2 * first + h, count, stride=2), :] for h in range(2)], axis=1
        )

    def put_rows(ref, first, count, value):
        for h in range(2):
            ref[pl.ds(2 * first + h, count, stride=2), :] = value[:, h * half : (h + 1) * half]

    side = 4
    last = tiles - 1

    def distance(k):
        return jnp.where(k == 0, 2, jnp.where(k == side - 1, 0, 2 * k - 1))

    def shifted(n, sign):
        y = lax.rem(tile // side + sign * distance(n // side) + side, side)
        x = lax.rem(lax.rem(tile, side) + sign * distance(lax.rem(n, side)) + side, side)
        return y * side + x

    load_chunks = 4
    chunk = cells // load_chunks

    def load(k):
        part = pl.ds(k * chunk, chunk)
        return pltpu.make_async_copy(state_ref.at[0, part], rows_bf.at[part], load_sem.at[k])

    small = [
        pltpu.make_async_copy(source, target, small_sem.at[q])
        for q, (source, target) in enumerate(
            (
                (couple_rows_hbm, couple_rows_ref),
                (couple_count_hbm, couple_count_ref),
                (cycle_hbm, cycle_ref),
                (halo_rows_hbm, halo_rows_ref),
                (halo_count_hbm, halo_count_ref),
                (couple_land_hbm, couple_land_ref),
                (couple_weight_hbm, couple_weight_ref),
                (dw_hbm, dw_ref),
                (gain_hbm, gain_ref),
                (up_hbm, up_ref),
                (bias_hbm, bias_ref),
                (down_hbm, down_ref),
            )
        )
    ]
    for k in range(load_chunks):
        load(k).start()
    for copy in small:
        copy.start()

    barrier = pltpu.get_barrier_semaphore()

    def greet(n, carry):
        pl.semaphore_signal(
            barrier, inc=1, device_id=place(comp, face, shifted(n, 1)), device_id_type=MESH
        )
        return carry

    lax.fori_loop(0, last, greet, 0)
    for target in (place(other, face, tile), near[2], near[3]):
        pl.semaphore_signal(barrier, inc=1, device_id=target, device_id_type=MESH)

    rows[pl.ds(2 * cells, 16), :] = jnp.zeros((16, half), F32)
    for k in range(load_chunks):
        load(k).wait()

        def widen(i, carry, k=k):
            first = k * chunk + i * 256
            part = pl.ds(pl.multiple_of(first, 256), 256)
            put_rows(rows, first, 256, rows_bf[part, :].astype(F32))
            return carry

        lax.fori_loop(0, chunk // 256, widen, 0)

    for copy in small[:9]:
        copy.wait()
    pl.semaphore_wait(barrier, last + 3)

    def cycle_copy(d):
        return pltpu.make_async_remote_copy(
            src_ref=cycle_ref,
            dst_ref=cycle_near.at[d],
            send_sem=cycle_send_sem.at[d],
            recv_sem=cycle_recv_sem.at[d],
            device_id=near[d ^ 1],
            device_id_type=MESH,
        )

    for d in range(4):
        cycle_copy(d).start()

    def slot_rows(n):
        return pl.ds(pl.multiple_of(n * slots, slots), slots)

    def cross_copy(n):
        own = isinstance(n, int) and n == last
        return pltpu.make_async_remote_copy(
            src_ref=send_rows.at[slot_rows(n)],
            dst_ref=(recv_rows if own else via_rows).at[slot_rows(n)],
            send_sem=cross_send_sem.at[n],
            recv_sem=cross_recv_sem.at[n],
            device_id=place(other, face, tile),
            device_id_type=MESH,
        )

    def pass_copy(n):
        return pltpu.make_async_remote_copy(
            src_ref=via_rows.at[slot_rows(n)],
            dst_ref=recv_rows.at[slot_rows(n)],
            send_sem=pass_send_sem.at[n],
            recv_sem=pass_recv_sem.at[n],
            device_id=place(comp, face, shifted(n, 1)),
            device_id_type=MESH,
        )

    def gather_send(n, carry):
        dest = shifted(n, 1)
        live = couple_count_ref[0, dest]
        step = 64

        def pick(g, inner):
            base = pl.multiple_of(g * step, step)
            index = [
                jnp.where(base + u < live, couple_rows_ref[0, dest, base + u], cells)
                for u in range(step)
            ]
            values = [rows[pl.ds(2 * i, 2), :] for i in index]
            for u in range(step):
                picked[pl.ds(pl.multiple_of(2 * base, 2 * step) + 2 * u, 2), :] = values[u]
            return inner

        lax.fori_loop(0, slots // step, pick, 0)
        send_rows[slot_rows(n), :] = get_rows(picked, 0, slots).astype(BF16)
        cross_copy(n).start()
        return carry

    lax.fori_loop(0, last, gather_send, 0)
    gather_send(last, 0)

    for d in range(4):
        cycle_copy(d).wait()
    index_i32[...] = jnp.full(index_i32.shape, cells, jnp.int32)
    groups = rim_rows // 128
    sub = lax.broadcasted_iota(jnp.int32, (128, cycle_len), 0)
    for d in range(4):
        table = jnp.transpose(
            jnp.concatenate(
                [halo_rows_ref[0, d : d + 1, 128 * g : 128 * (g + 1)] for g in range(groups)], axis=0
            )
        )
        slot = cycle_near[d] - d * rim_rows
        group = jnp.right_shift(slot, 7)
        found = jnp.zeros((128, cycle_len), jnp.int32)
        for g in range(groups):
            found = jnp.where(group == g, table[:, g : g + 1], found)
        found = jnp.where(jnp.bitwise_and(slot, 127) == sub, found, 0)
        found = sum(found[8 * k : 8 * k + 8] for k in range(16))
        row = sum(found[k : k + 1] for k in range(8))
        live = (slot >= 0) & (slot < halo_count_ref[0, d])
        index_i32[d : d + 1, pl.ds(0, cycle_len)] = jnp.where(live, row, cells)
    to_smem = pltpu.make_async_copy(index_i32, index_smem, smem_sem)
    to_smem.start()
    index_col[...] = jnp.transpose(index_i32[...].astype(F32))

    pair = 2 * slots
    pairs = tiles // 2
    early = pairs - 4
    lane_col = lax.broadcasted_iota(jnp.int32, (GRID_W, pair), 0)

    def forward(n):
        cross_copy(n).wait_recv()
        pass_copy(n).start()

    def project(p):
        part = pl.ds(pl.multiple_of(p * pair, pair), pair)
        value = jnp.dot(recv_rows[part, :], couple_weight_ref[0], preferred_element_type=F32)
        arrived[lax.rem(p, 4)] = value.astype(BF16)

    def land_lanes(p):
        return jnp.concatenate(
            [couple_land_ref[0, pl.ds(shifted(2 * p + q, -1), 1), :] for q in range(2)], axis=1
        )

    def landed(p):
        land = land_lanes(p)
        land_row = jnp.right_shift(land, 7)
        in_col = jnp.where(jnp.bitwise_and(land, GRID_W - 1) == lane_col, 1.0, 0.0).astype(BF16)
        hot = jnp.concatenate(
            [in_col * jnp.where(land_row == i, 1.0, 0.0).astype(BF16) for i in range(height)], axis=0
        )
        added = jnp.dot(hot, arrived[lax.rem(p, 4)], preferred_element_type=F32)
        return get_rows(rows, 0, cells) + added

    def land_pair(p):
        pass_copy(2 * p).wait_recv()
        pass_copy(2 * p + 1).wait_recv()
        project(p)
        put_rows(rows, 0, cells, landed(p))

    step = 92

    def pick_halo(d):
        def pick(g, carry):
            values = [
                rows[pl.ds(2 * index_smem[d, g * step + u], 2), :] for u in range(step)
            ]
            start = pl.multiple_of(2 * (d * border_rows + g * step), 2 * step)
            for u in range(step):
                halo_part[pl.ds(start + 2 * u, 2), :] = values[u]
            return carry

        lax.fori_loop(0, border_rows // step, pick, 0)

    forward(0)
    forward(1)

    def early_step(p, carry):
        forward(2 * p)
        forward(2 * p + 1)
        land_pair(p - 1)
        return carry

    lax.fori_loop(1, early + 1, early_step, 0)
    to_smem.wait()

    def pick_step(d, carry):
        pick_halo(d)
        forward(2 * early + 2 + d)
        return carry

    lax.fori_loop(0, 4, pick_step, 0)

    def late_step(p, carry):
        land_pair(p)
        return carry

    lax.fori_loop(early, early + 1, late_step, 0)
    forward(last - 1)
    lax.fori_loop(early + 1, pairs - 1, late_step, 0)
    cross_copy(last).wait_recv()
    pass_copy(last - 1).wait_recv()

    project(pairs - 1)

    def halo_copy(d):
        return pltpu.make_async_remote_copy(
            src_ref=halo_send.at[d],
            dst_ref=halo_recv.at[d],
            send_sem=halo_send_sem.at[d],
            recv_sem=halo_recv_sem.at[d],
            device_id=near[d],
            device_id_type=MESH,
        )

    late_land = jnp.concatenate([land_lanes(p) for p in range(early, pairs)], axis=1).astype(F32)
    late_rows = jnp.concatenate([arrived[p % 4] for p in range(early, pairs)], axis=0)
    for d in (2, 3, 0, 1):
        hot = jnp.where(index_col[pl.ds(0, border_rows), d : d + 1] == late_land, 1.0, 0.0).astype(BF16)
        value = get_rows(halo_part, d * border_rows, border_rows) + jnp.dot(
            hot, late_rows, preferred_element_type=F32
        )
        halo_send[d] = value.astype(BF16)
        halo_copy(d).start()

    joined = landed(pairs - 1).astype(BF16)
    rows_bf[...] = joined
    put_rows(rows, 0, cells, joined.astype(F32))

    taps = [dw_ref[q] for q in range(9)]
    gain = gain_ref[...]

    def mix(above, here, below):
        left, mid, right = (
            taps[c] * above + taps[3 + c] * here + taps[6 + c] * below for c in range(3)
        )
        return mid + pltpu.roll(left, 1, 0) + pltpu.roll(right, GRID_W - 1, 0)

    def grid_row(i):
        return get_rows(rows, i * GRID_W, GRID_W)

    band = 8
    bands = height // band

    def interior(b, carry):
        for q in range(band):
            i = b * band + q
            mixed = mix(
                grid_row(jnp.maximum(i - 1, 0)), grid_row(i), grid_row(jnp.minimum(i + 1, height - 1))
            )
            part = pl.ds(pl.multiple_of(i * GRID_W, GRID_W), GRID_W)
            normed[part, :] = norm(mixed, gain).astype(BF16)
        return carry

    lax.fori_loop(0, bands, interior, 0)

    for copy in small[9:]:
        copy.wait()
    down = (0.5 * down_ref[0].astype(F32)).astype(BF16)

    def mlp(value):
        before = jnp.dot(value, up_ref[0], preferred_element_type=F32) + bias_ref[...]
        return jnp.dot(twice_gelu(before).astype(BF16), down, preferred_element_type=F32)

    def level(first, size):
        part = pl.ds(first, size)
        out[part, :] = (rows_bf[part, :].astype(F32) + mlp(normed[part, :])).astype(BF16)

    def store(k, first, size):
        part = pl.ds(first, size)
        return pltpu.make_async_copy(out.at[part], out_hbm.at[0, part], store_sem.at[k])

    block = 1024
    ahead = 3 * block
    for first in range(0, ahead, block):
        level(first, block)

    outer = ((1, 0), (2, 1), (3, GRID_W - 2), (4, GRID_W - 1))

    for q, col in outer:
        for h in range(2):
            column = rows[pl.ds(2 * col + h, height, stride=2 * GRID_W), :]
            columns[q, pl.ds(1, height), pl.ds(h * half, half)] = column
    for d in range(4):
        halo_copy(d).wait_recv()

    border[...] = (halo_recv[0].astype(F32) + halo_recv[1].astype(F32)) + (
        halo_recv[2].astype(F32) + halo_recv[3].astype(F32)
    )
    wide = GRID_W + 2
    for q, col in outer:
        columns[q, pl.ds(0, 1), :] = border[pl.ds(1 + col, 1), :]
        columns[q, pl.ds(height + 1, 1), :] = border[pl.ds(wide + 1 + col, 1), :]
    for q, corner, side in ((0, 0, 2 * wide), (5, wide - 1, 2 * wide + height)):
        columns[q, pl.ds(0, 1), :] = border[pl.ds(corner, 1), :]
        columns[q, pl.ds(1, height), :] = border[pl.ds(side, height), :]
        columns[q, pl.ds(height + 1, 1), :] = border[pl.ds(wide + corner, 1), :]
    mixed = [
        mix(border[pl.ds(1, GRID_W), :], grid_row(0), grid_row(1)),
        mix(grid_row(height - 2), grid_row(height - 1), border[pl.ds(wide + 1, GRID_W), :]),
    ]
    for first in (0, 3):
        total = None
        for r in range(3):
            for c in range(3):
                term = taps[3 * r + c] * columns[first + c, pl.ds(r, height), :]
                total = term if total is None else total + term
        mixed.append(total)
    edges = norm(jnp.concatenate(mixed, axis=0), gain)
    line = lax.broadcasted_iota(jnp.int32, (TILE, channels), 0)

    def merge(ref, i, left, right):
        for fresh, first, at in ((left, 0, 0), (right, GRID_W - TILE, TILE - 1)):
            box = pl.ds(i * GRID_W + first, TILE)
            fixed = jnp.where(line == at, fresh, ref[box, :].astype(F32))
            ref[box, :] = fixed.astype(BF16)

    lefts, rights = 2 * GRID_W, 2 * GRID_W + height
    normed[pl.ds(cells - GRID_W, GRID_W), :] = edges[GRID_W : 2 * GRID_W].astype(BF16)
    first_row = ahead // GRID_W
    for i in range(first_row, height):
        merge(normed, i, edges[lefts + i : lefts + i + 1], edges[rights + i : rights + i + 1])
    value = jnp.concatenate(
        [edges[:GRID_W], edges[lefts : lefts + first_row], edges[rights : rights + first_row]], axis=0
    )
    around = jnp.concatenate(
        [rows_bf[pl.ds(0, GRID_W), :].astype(F32)]
        + [columns[q, pl.ds(1, first_row), :] for q in (1, 4)],
        axis=0,
    )
    fresh = around + mlp(value.astype(BF16))
    out[pl.ds(0, GRID_W), :] = fresh[:GRID_W].astype(BF16)
    for i in range(first_row):
        left = GRID_W + i
        right = left + first_row
        merge(out, i, fresh[left : left + 1], fresh[right : right + 1])
    stores = [store(0, 0, ahead)]
    stores[0].start()
    for first in range(ahead, cells, block):
        level(first, block)
        stores.append(store(len(stores), first, block))
        stores[-1].start()

    for n in range(tiles):
        cross_copy(n).wait_send()
    for n in range(last):
        pass_copy(n).wait_send()
    for d in range(4):
        halo_copy(d).wait_send()
    for copy in stores:
        copy.wait()


def twice_gelu(before):
    inner = before * (0.7978845608028654 + 0.035677408136300125 * (before * before))
    return before + before * jnp.tanh(inner)


def body(
    state,
    cycle_source,
    halo_rows,
    halo_count,
    couple_rows,
    couple_count,
    couple_land,
    couple_weight,
    dw_weight,
    norm_gain,
    up_weight,
    up_bias,
    down_weight,
):
    _, cells, channels = state.shape
    tiles, faces = lax.axis_size("tile"), lax.axis_size("face")
    cycle_len = cycle_source.shape[1]
    border_rows = -(-cycle_len // TILE) * TILE
    index_lanes = -(-cycle_len // 128) * 128
    slots = couple_rows.shape[2]
    height = cells // GRID_W
    hbm = pl.BlockSpec(memory_space=pl.ANY)
    dma = pltpu.SemaphoreType.DMA
    vmem = pltpu.VMEM
    return pl.pallas_call(
        functools.partial(couple_kernel, tiles, faces, cycle_len),
        name="couple_and_mix",
        out_shape=jax.ShapeDtypeStruct((1, cells, channels), BF16),
        in_specs=[hbm] * 13,
        out_specs=hbm,
        scratch_shapes=[
            vmem((1, cycle_len), jnp.int32),
            vmem(halo_rows.shape, jnp.int32),
            pltpu.SMEM((1, 4), jnp.int32),
            pltpu.SMEM(couple_rows.shape, jnp.int32),
            pltpu.SMEM((1, tiles), jnp.int32),
            vmem(couple_land.shape, jnp.int32),
            vmem(couple_weight.shape, BF16),
            vmem((9, 1, channels), F32),
            vmem((1, channels), F32),
            vmem(up_weight.shape, BF16),
            vmem(up_bias.shape, F32),
            vmem(down_weight.shape, BF16),
            vmem((cells, channels), BF16),
            vmem((2 * cells + 16, channels // 2), F32),
            vmem((2 * slots, channels // 2), F32),
            vmem((tiles * slots, channels), BF16),
            vmem((tiles * slots, channels), BF16),
            vmem((tiles * slots, channels), BF16),
            vmem((4, 2 * slots, channels), BF16),
            vmem((4, 1, cycle_len), jnp.int32),
            vmem((8, index_lanes), jnp.int32),
            pltpu.SMEM((8, index_lanes), jnp.int32),
            vmem((index_lanes, 8), F32),
            vmem((4 * 2 * border_rows, channels // 2), F32),
            vmem((4, border_rows, channels), BF16),
            vmem((4, border_rows, channels), BF16),
            vmem((border_rows, channels), F32),
            vmem((6, height + 8, channels), F32),
            vmem((cells, channels), BF16),
            vmem((cells, channels), BF16),
            dma((4,)),
            dma((12,)),
            dma,
            dma((4,)),
            dma((tiles,)),
            dma((tiles,)),
            dma((tiles,)),
            dma((tiles,)),
            dma((4,)),
            dma((4,)),
            dma((4,)),
            dma((4,)),
        ],
        compiler_params=pltpu.CompilerParams(
            collective_id=0, has_side_effects=True, vmem_limit_bytes=64 << 20
        ),
    )(
        state,
        cycle_source,
        halo_rows,
        halo_count.reshape(1, 4),
        couple_rows,
        couple_count.reshape(1, tiles),
        couple_land,
        couple_weight,
        jnp.transpose(dw_weight, (1, 0, 2)),
        norm_gain,
        up_weight,
        up_bias,
        down_weight,
    )


def solution(mesh):
    in_specs = (
        P("comp", ("face", "tile"), None),
        P("comp", ("face", "tile")),
        P("comp", None, ("face", "tile")),
        P("comp", None, ("face", "tile")),
        P("comp", None, ("face", "tile")),
        P("comp", None, ("face", "tile")),
        P("comp", None, ("face", "tile")),
        P("comp", None, None),
        P("comp", None, None),
        P("comp", None),
        P("comp", None, None),
        P("comp", None),
        P("comp", None, None),
    )
    out_specs = P("comp", ("face", "tile"), None)
    return jax.shard_map(body, mesh=mesh, in_specs=in_specs, out_specs=out_specs, check_vma=False)
```

```python
import functools

import jax
import jax.numpy as jnp
from jax import lax
from jax.experimental import pallas as pl
from jax.experimental.pallas import tpu as pltpu
from jax.sharding import PartitionSpec as P

MESH = pl.DeviceIdType.MESH
GRID_W = 128
F32 = jnp.float32
BF16 = jnp.bfloat16
TILE = 16


def place(comp, face, tile):
    return {"comp": comp, "face": face, "tile": tile}


def norm(mixed, gain):
    center = mixed - jnp.mean(mixed, axis=-1, keepdims=True)
    spread = jnp.mean(center * center, axis=-1, keepdims=True)
    return center * lax.rsqrt(spread + 1e-06) * gain


def couple_kernel(
    tiles,
    faces,
    cycle_len,
    state_ref,
    cycle_hbm,
    halo_rows_hbm,
    halo_count_hbm,
    couple_rows_hbm,
    couple_count_hbm,
    couple_land_hbm,
    couple_weight_hbm,
    dw_hbm,
    gain_hbm,
    up_hbm,
    bias_hbm,
    down_hbm,
    out_hbm,
    cycle_ref,
    halo_rows_ref,
    halo_count_ref,
    couple_rows_ref,
    couple_count_ref,
    couple_land_ref,
    couple_weight_ref,
    dw_ref,
    gain_ref,
    up_ref,
    bias_ref,
    down_ref,
    rows_bf,
    rows,
    picked,
    send_rows,
    via_rows,
    recv_rows,
    arrived,
    cycle_near,
    index_i32,
    index_smem,
    index_col,
    halo_part,
    halo_send,
    halo_recv,
    border,
    columns,
    normed,
    out,
    load_sem,
    small_sem,
    smem_sem,
    store_sem,
    cross_send_sem,
    cross_recv_sem,
    pass_send_sem,
    pass_recv_sem,
    cycle_send_sem,
    cycle_recv_sem,
    halo_send_sem,
    halo_recv_sem,
):
    comp, face, tile = lax.axis_index("comp"), lax.axis_index("face"), lax.axis_index("tile")
    cells, channels = rows_bf.shape
    half = channels // 2
    height = cells // GRID_W
    slots = couple_rows_ref.shape[2]
    rim_rows = halo_rows_ref.shape[2]
    border_rows = halo_send.shape[1]
    other = 1 - comp
    near = [
        place(comp, face, lax.rem(tile + 1, tiles)),
        place(comp, face, lax.rem(tile + tiles - 1, tiles)),
        place(comp, lax.rem(face + 1, faces), tile),
        place(comp, lax.rem(face + faces - 1, faces), tile),
    ]

    def get_rows(ref, first, count):
        return jnp.concatenate(
            [ref[pl.ds(2 * first + h, count, stride=2), :] for h in range(2)], axis=1
        )

    def put_rows(ref, first, count, value):
        for h in range(2):
            ref[pl.ds(2 * first + h, count, stride=2), :] = value[:, h * half : (h + 1) * half]

    side = 4
    last = tiles - 1

    def distance(k):
        return jnp.where(k == 0, 0, jnp.where(k == 1, 3, k - 1))

    def shifted(n, sign):
        y = lax.rem(tile // side + sign * distance(n // side) + side, side)
        x = lax.rem(lax.rem(tile, side) + sign * distance(lax.rem(n, side)) + side, side)
        return y * side + x

    load_chunks = 4
    chunk = cells // load_chunks

    def load(k):
        part = pl.ds(k * chunk, chunk)
        return pltpu.make_async_copy(state_ref.at[0, part], rows_bf.at[part], load_sem.at[k])

    small = [
        pltpu.make_async_copy(source, target, small_sem.at[q])
        for q, (source, target) in enumerate(
            (
                (couple_rows_hbm, couple_rows_ref),
                (couple_count_hbm, couple_count_ref),
                (cycle_hbm, cycle_ref),
                (halo_rows_hbm, halo_rows_ref),
                (halo_count_hbm, halo_count_ref),
                (couple_land_hbm, couple_land_ref),
                (couple_weight_hbm, couple_weight_ref),
                (dw_hbm, dw_ref),
                (gain_hbm, gain_ref),
                (up_hbm, up_ref),
                (bias_hbm, bias_ref),
                (down_hbm, down_ref),
            )
        )
    ]
    for k in range(load_chunks):
        load(k).start()
    for copy in small:
        copy.start()

    barrier = pltpu.get_barrier_semaphore()

    def greet(n, carry):
        pl.semaphore_signal(
            barrier, inc=1, device_id=place(comp, face, shifted(n, 1)), device_id_type=MESH
        )
        return carry

    lax.fori_loop(1, tiles, greet, 0)
    for target in (place(other, face, tile), near[2], near[3]):
        pl.semaphore_signal(barrier, inc=1, device_id=target, device_id_type=MESH)

    rows[pl.ds(2 * cells, 16), :] = jnp.zeros((16, half), F32)
    for k in range(load_chunks):
        load(k).wait()

        def widen(i, carry, k=k):
            first = k * chunk + i * 256
            part = pl.ds(pl.multiple_of(first, 256), 256)
            put_rows(rows, first, 256, rows_bf[part, :].astype(F32))
            return carry

        lax.fori_loop(0, chunk // 256, widen, 0)

    for copy in small[:9]:
        copy.wait()
    pl.semaphore_wait(barrier, last + 3)

    def cycle_copy(d):
        return pltpu.make_async_remote_copy(
            src_ref=cycle_ref,
            dst_ref=cycle_near.at[d],
            send_sem=cycle_send_sem.at[d],
            recv_sem=cycle_recv_sem.at[d],
            device_id=near[d ^ 1],
            device_id_type=MESH,
        )

    for d in range(4):
        cycle_copy(d).start()

    def slot_rows(n):
        return pl.ds(pl.multiple_of(n * slots, slots), slots)

    def pass_copy(n):
        return pltpu.make_async_remote_copy(
            src_ref=send_rows.at[slot_rows(n)],
            dst_ref=via_rows.at[slot_rows(n)],
            send_sem=pass_send_sem.at[n],
            recv_sem=pass_recv_sem.at[n],
            device_id=place(comp, face, shifted(n, 1)),
            device_id_type=MESH,
        )

    def cross_copy(n):
        own = isinstance(n, int) and n == 0
        return pltpu.make_async_remote_copy(
            src_ref=(send_rows if own else via_rows).at[slot_rows(n)],
            dst_ref=recv_rows.at[slot_rows(n)],
            send_sem=cross_send_sem.at[n],
            recv_sem=cross_recv_sem.at[n],
            device_id=place(other, face, tile),
            device_id_type=MESH,
        )

    def gather(n):
        dest = shifted(n, 1)
        live = couple_count_ref[0, dest]
        step = slots

        def pick(g, inner):
            base = pl.multiple_of(g * step, step)
            index = [
                jnp.where(base + u < live, couple_rows_ref[0, dest, base + u], cells)
                for u in range(step)
            ]
            values = [rows[pl.ds(2 * i, 2), :] for i in index]
            for u in range(step):
                picked[pl.ds(pl.multiple_of(2 * base, 2 * step) + 2 * u, 2), :] = values[u]
            return inner

        lax.fori_loop(0, slots // step, pick, 0)
        send_rows[slot_rows(n), :] = get_rows(picked, 0, slots).astype(BF16)

    def gather_send(n, carry):
        gather(n)
        pass_copy(n).start()
        return carry

    gather(0)
    cross_copy(0).start()
    lax.fori_loop(1, tiles, gather_send, 0)

    for d in range(4):
        cycle_copy(d).wait()
    index_i32[...] = jnp.full(index_i32.shape, cells, jnp.int32)
    groups = rim_rows // 128
    sub = lax.broadcasted_iota(jnp.int32, (128, cycle_len), 0)
    for d in range(4):
        table = jnp.transpose(
            jnp.concatenate(
                [halo_rows_ref[0, d : d + 1, 128 * g : 128 * (g + 1)] for g in range(groups)], axis=0
            )
        )
        slot = cycle_near[d] - d * rim_rows
        group = jnp.right_shift(slot, 7)
        found = jnp.zeros((128, cycle_len), jnp.int32)
        for g in range(groups):
            found = jnp.where(group == g, table[:, g : g + 1], found)
        found = jnp.where(jnp.bitwise_and(slot, 127) == sub, found, 0)
        found = sum(found[8 * k : 8 * k + 8] for k in range(16))
        row = sum(found[k : k + 1] for k in range(8))
        live = (slot >= 0) & (slot < halo_count_ref[0, d])
        index_i32[d : d + 1, pl.ds(0, cycle_len)] = jnp.where(live, row, cells)
    to_smem = pltpu.make_async_copy(index_i32, index_smem, smem_sem)
    to_smem.start()
    turned = jnp.transpose(index_i32[...].astype(F32))
    for d in range(4):
        index_col[pl.ds(d * border_rows, border_rows), :] = jnp.broadcast_to(
            turned[:border_rows, d : d + 1], (border_rows, 128)
        )

    def forward(n, carry):
        pass_copy(n).wait_recv()
        cross_copy(n).start()
        return carry

    lax.fori_loop(1, tiles, forward, 0)

    pair = 2 * slots
    pairs = tiles // 2
    early = pairs - 3
    lane_col = lax.broadcasted_iota(jnp.int32, (GRID_W, pair), 0)

    def project(p):
        part = pl.ds(pl.multiple_of(p * pair, pair), pair)
        value = jnp.dot(recv_rows[part, :], couple_weight_ref[0], preferred_element_type=F32)
        arrived[p] = value.astype(BF16)

    def land_lanes(p):
        return jnp.concatenate(
            [couple_land_ref[0, pl.ds(shifted(2 * p + q, -1), 1), :] for q in range(2)], axis=1
        )

    def landed(p):
        land = land_lanes(p)
        land_row = jnp.right_shift(land, 7)
        in_col = jnp.where(jnp.bitwise_and(land, GRID_W - 1) == lane_col, 1.0, 0.0).astype(BF16)
        hot = jnp.concatenate(
            [in_col * jnp.where(land_row == i, 1.0, 0.0).astype(BF16) for i in range(height)], axis=0
        )
        added = jnp.dot(hot, arrived[p], preferred_element_type=F32)
        return get_rows(rows, 0, cells) + added

    def land_pair(p):
        cross_copy(2 * p).wait_recv()
        cross_copy(2 * p + 1).wait_recv()
        project(p)
        put_rows(rows, 0, cells, landed(p))

    step = 92

    def pick_halo(d):
        def pick(g, carry):
            values = [
                rows[pl.ds(2 * index_smem[d, g * step + u], 2), :] for u in range(step)
            ]
            start = pl.multiple_of(2 * (d * border_rows + g * step), 2 * step)
            for u in range(step):
                halo_part[pl.ds(start + 2 * u, 2), :] = values[u]
            return carry

        lax.fori_loop(0, border_rows // step, pick, 0)

    def land_step(p, carry):
        land_pair(p)
        return carry

    lax.fori_loop(0, early, land_step, 0)
    to_smem.wait()

    def pick_step(d, carry):
        pick_halo(d)
        return carry

    lax.fori_loop(0, 4, pick_step, 0)
    lax.fori_loop(early, pairs - 1, land_step, 0)
    cross_copy(last - 1).wait_recv()
    cross_copy(last).wait_recv()

    project(pairs - 1)

    def halo_copy(d):
        return pltpu.make_async_remote_copy(
            src_ref=halo_send.at[d],
            dst_ref=halo_recv.at[d],
            send_sem=halo_send_sem.at[d],
            recv_sem=halo_recv_sem.at[d],
            device_id=near[d],
            device_id_type=MESH,
        )

    late_land = jnp.concatenate([land_lanes(p) for p in range(early, pairs)], axis=1).astype(F32)
    late_rows = jnp.concatenate([arrived[p] for p in range(early, pairs)], axis=0)
    for d in (2, 0):
        wanted = index_col[pl.ds(d * border_rows, 2 * border_rows), :]
        hot = jnp.concatenate(
            [
                jnp.where(wanted == late_land[:, 128 * k : 128 * (k + 1)], 1.0, 0.0).astype(BF16)
                for k in range(late_land.shape[1] // 128)
            ],
            axis=1,
        )
        value = get_rows(halo_part, d * border_rows, 2 * border_rows) + jnp.dot(
            hot, late_rows, preferred_element_type=F32
        )
        for q in range(2):
            halo_send[d + q] = value[q * border_rows : (q + 1) * border_rows].astype(BF16)
            halo_copy(d + q).start()

    joined = landed(pairs - 1).astype(BF16)
    rows_bf[...] = joined
    put_rows(rows, 0, cells, joined.astype(F32))

    taps = [dw_ref[q] for q in range(9)]
    gain = gain_ref[...]

    def mix(above, here, below):
        left, mid, right = (
            taps[c] * above + taps[3 + c] * here + taps[6 + c] * below for c in range(3)
        )
        return mid + pltpu.roll(left, 1, 0) + pltpu.roll(right, GRID_W - 1, 0)

    def grid_row(i):
        return get_rows(rows, i * GRID_W, GRID_W)

    band = 8
    bands = height // band

    def interior(b, carry):
        for q in range(band):
            i = b * band + q
            mixed = mix(
                grid_row(jnp.maximum(i - 1, 0)), grid_row(i), grid_row(jnp.minimum(i + 1, height - 1))
            )
            part = pl.ds(pl.multiple_of(i * GRID_W, GRID_W), GRID_W)
            normed[part, :] = norm(mixed, gain).astype(BF16)
        return carry

    lax.fori_loop(0, bands, interior, 0)

    for copy in small[9:]:
        copy.wait()
    down = (0.5 * down_ref[0].astype(F32)).astype(BF16)

    def mlp(value):
        before = jnp.dot(value, up_ref[0], preferred_element_type=F32) + bias_ref[...]
        return jnp.dot(twice_gelu(before).astype(BF16), down, preferred_element_type=F32)

    def level(first, size):
        part = pl.ds(first, size)
        out[part, :] = (rows_bf[part, :].astype(F32) + mlp(normed[part, :])).astype(BF16)

    def store(k, first, size):
        part = pl.ds(first, size)
        return pltpu.make_async_copy(out.at[part], out_hbm.at[0, part], store_sem.at[k])

    block = 1024
    ahead = 3 * block
    for first in range(0, ahead, block):
        level(first, block)

    outer = ((1, 0), (2, 1), (3, GRID_W - 2), (4, GRID_W - 1))

    for q, col in outer:
        for h in range(2):
            column = rows[pl.ds(2 * col + h, height, stride=2 * GRID_W), :]
            columns[q, pl.ds(1, height), pl.ds(h * half, half)] = column
    for d in range(4):
        halo_copy(d).wait_recv()

    border[...] = (halo_recv[0].astype(F32) + halo_recv[1].astype(F32)) + (
        halo_recv[2].astype(F32) + halo_recv[3].astype(F32)
    )
    wide = GRID_W + 2
    for q, col in outer:
        columns[q, pl.ds(0, 1), :] = border[pl.ds(1 + col, 1), :]
        columns[q, pl.ds(height + 1, 1), :] = border[pl.ds(wide + 1 + col, 1), :]
    for q, corner, side in ((0, 0, 2 * wide), (5, wide - 1, 2 * wide + height)):
        columns[q, pl.ds(0, 1), :] = border[pl.ds(corner, 1), :]
        columns[q, pl.ds(1, height), :] = border[pl.ds(side, height), :]
        columns[q, pl.ds(height + 1, 1), :] = border[pl.ds(wide + corner, 1), :]
    mixed = [
        mix(border[pl.ds(1, GRID_W), :], grid_row(0), grid_row(1)),
        mix(grid_row(height - 2), grid_row(height - 1), border[pl.ds(wide + 1, GRID_W), :]),
    ]
    for first in (0, 3):
        total = None
        for r in range(3):
            for c in range(3):
                term = taps[3 * r + c] * columns[first + c, pl.ds(r, height), :]
                total = term if total is None else total + term
        mixed.append(total)
    edges = norm(jnp.concatenate(mixed, axis=0), gain)
    line = lax.broadcasted_iota(jnp.int32, (TILE, channels), 0)

    def merge(ref, i, left, right):
        for fresh, first, at in ((left, 0, 0), (right, GRID_W - TILE, TILE - 1)):
            box = pl.ds(i * GRID_W + first, TILE)
            fixed = jnp.where(line == at, fresh, ref[box, :].astype(F32))
            ref[box, :] = fixed.astype(BF16)

    lefts, rights = 2 * GRID_W, 2 * GRID_W + height
    normed[pl.ds(cells - GRID_W, GRID_W), :] = edges[GRID_W : 2 * GRID_W].astype(BF16)
    first_row = ahead // GRID_W
    for i in range(first_row, height):
        merge(normed, i, edges[lefts + i : lefts + i + 1], edges[rights + i : rights + i + 1])
    value = jnp.concatenate(
        [edges[:GRID_W], edges[lefts : lefts + first_row], edges[rights : rights + first_row]], axis=0
    )
    around = jnp.concatenate(
        [rows_bf[pl.ds(0, GRID_W), :].astype(F32)]
        + [columns[q, pl.ds(1, first_row), :] for q in (1, 4)],
        axis=0,
    )
    fresh = around + mlp(value.astype(BF16))
    out[pl.ds(0, GRID_W), :] = fresh[:GRID_W].astype(BF16)
    for i in range(first_row):
        left = GRID_W + i
        right = left + first_row
        merge(out, i, fresh[left : left + 1], fresh[right : right + 1])
    stores = [store(0, 0, ahead)]
    stores[0].start()
    for first in range(ahead, cells, block):
        level(first, block)
        stores.append(store(len(stores), first, block))
        stores[-1].start()

    for n in range(tiles):
        cross_copy(n).wait_send()
    for n in range(1, tiles):
        pass_copy(n).wait_send()
    for d in range(4):
        halo_copy(d).wait_send()
    for copy in stores:
        copy.wait()


def twice_gelu(before):
    inner = before * (0.7978845608028654 + 0.035677408136300125 * (before * before))
    return before + before * jnp.tanh(inner)


def body(
    state,
    cycle_source,
    halo_rows,
    halo_count,
    couple_rows,
    couple_count,
    couple_land,
    couple_weight,
    dw_weight,
    norm_gain,
    up_weight,
    up_bias,
    down_weight,
):
    _, cells, channels = state.shape
    tiles, faces = lax.axis_size("tile"), lax.axis_size("face")
    cycle_len = cycle_source.shape[1]
    border_rows = -(-cycle_len // TILE) * TILE
    index_lanes = -(-cycle_len // 128) * 128
    slots = couple_rows.shape[2]
    height = cells // GRID_W
    hbm = pl.BlockSpec(memory_space=pl.ANY)
    dma = pltpu.SemaphoreType.DMA
    vmem = pltpu.VMEM
    return pl.pallas_call(
        functools.partial(couple_kernel, tiles, faces, cycle_len),
        name="couple_and_mix",
        out_shape=jax.ShapeDtypeStruct((1, cells, channels), BF16),
        in_specs=[hbm] * 13,
        out_specs=hbm,
        scratch_shapes=[
            vmem((1, cycle_len), jnp.int32),
            vmem(halo_rows.shape, jnp.int32),
            pltpu.SMEM((1, 4), jnp.int32),
            pltpu.SMEM(couple_rows.shape, jnp.int32),
            pltpu.SMEM((1, tiles), jnp.int32),
            vmem(couple_land.shape, jnp.int32),
            vmem(couple_weight.shape, BF16),
            vmem((9, 1, channels), F32),
            vmem((1, channels), F32),
            vmem(up_weight.shape, BF16),
            vmem(up_bias.shape, F32),
            vmem(down_weight.shape, BF16),
            vmem((cells, channels), BF16),
            vmem((2 * cells + 16, channels // 2), F32),
            vmem((2 * slots, channels // 2), F32),
            vmem((tiles * slots, channels), BF16),
            vmem((tiles * slots, channels), BF16),
            vmem((tiles * slots, channels), BF16),
            vmem((tiles // 2, 2 * slots, channels), BF16),
            vmem((4, 1, cycle_len), jnp.int32),
            vmem((8, index_lanes), jnp.int32),
            pltpu.SMEM((8, index_lanes), jnp.int32),
            vmem((4 * border_rows, 128), F32),
            vmem((4 * 2 * border_rows, channels // 2), F32),
            vmem((4, border_rows, channels), BF16),
            vmem((4, border_rows, channels), BF16),
            vmem((border_rows, channels), F32),
            vmem((6, height + 8, channels), F32),
            vmem((cells, channels), BF16),
            vmem((cells, channels), BF16),
            dma((4,)),
            dma((12,)),
            dma,
            dma((4,)),
            dma((tiles,)),
            dma((tiles,)),
            dma((tiles,)),
            dma((tiles,)),
            dma((4,)),
            dma((4,)),
            dma((4,)),
            dma((4,)),
        ],
        compiler_params=pltpu.CompilerParams(
            collective_id=0, has_side_effects=True, vmem_limit_bytes=64 << 20
        ),
    )(
        state,
        cycle_source,
        halo_rows,
        halo_count.reshape(1, 4),
        couple_rows,
        couple_count.reshape(1, tiles),
        couple_land,
        couple_weight,
        jnp.transpose(dw_weight, (1, 0, 2)),
        norm_gain,
        up_weight,
        up_bias,
        down_weight,
    )


def solution(mesh):
    in_specs = (
        P("comp", ("face", "tile"), None),
        P("comp", ("face", "tile")),
        P("comp", None, ("face", "tile")),
        P("comp", None, ("face", "tile")),
        P("comp", None, ("face", "tile")),
        P("comp", None, ("face", "tile")),
        P("comp", None, ("face", "tile")),
        P("comp", None, None),
        P("comp", None, None),
        P("comp", None),
        P("comp", None, None),
        P("comp", None),
        P("comp", None, None),
    )
    out_specs = P("comp", ("face", "tile"), None)
    return jax.shard_map(body, mesh=mesh, in_specs=in_specs, out_specs=out_specs, check_vma=False)
```

```python
import functools

import jax
import jax.numpy as jnp
from jax import lax
from jax.experimental import pallas as pl
from jax.experimental.pallas import tpu as pltpu
from jax.sharding import PartitionSpec as P

MESH = pl.DeviceIdType.MESH
GRID_W = 128
F32 = jnp.float32
BF16 = jnp.bfloat16
TILE = 16


def place(comp, face, tile):
    return {"comp": comp, "face": face, "tile": tile}


def norm(mixed, gain):
    center = mixed - jnp.mean(mixed, axis=-1, keepdims=True)
    spread = jnp.mean(center * center, axis=-1, keepdims=True)
    return center * lax.rsqrt(spread + 1e-06) * gain


def couple_kernel(
    tiles,
    faces,
    cycle_len,
    state_ref,
    cycle_hbm,
    halo_rows_hbm,
    halo_count_hbm,
    couple_rows_hbm,
    couple_count_hbm,
    couple_land_hbm,
    couple_weight_hbm,
    dw_hbm,
    gain_hbm,
    up_hbm,
    bias_hbm,
    down_hbm,
    out_hbm,
    cycle_ref,
    halo_rows_ref,
    halo_count_ref,
    couple_rows_ref,
    couple_count_ref,
    couple_land_ref,
    couple_weight_ref,
    dw_ref,
    gain_ref,
    up_ref,
    bias_ref,
    down_ref,
    rows_bf,
    rows_all,
    picked,
    send_rows,
    via_rows,
    recv_rows,
    arrived,
    cycle_near,
    index_i32,
    index_smem,
    index_col,
    halo_part,
    halo_send,
    halo_recv,
    border,
    columns,
    normed,
    out,
    load_sem,
    small_sem,
    smem_sem,
    store_sem,
    cross_send_sem,
    cross_recv_sem,
    pass_send_sem,
    pass_recv_sem,
    cycle_send_sem,
    cycle_recv_sem,
    halo_send_sem,
    halo_recv_sem,
):
    comp, face, tile = lax.axis_index("comp"), lax.axis_index("face"), lax.axis_index("tile")
    cells, channels = rows_bf.shape
    half = channels // 2
    height = cells // GRID_W
    slots = couple_rows_ref.shape[2]
    rim_rows = halo_rows_ref.shape[2]
    border_rows = halo_send.shape[1]
    other = 1 - comp
    near = [
        place(comp, face, lax.rem(tile + 1, tiles)),
        place(comp, face, lax.rem(tile + tiles - 1, tiles)),
        place(comp, lax.rem(face + 1, faces), tile),
        place(comp, lax.rem(face + faces - 1, faces), tile),
    ]

    margin = 16
    rows = rows_all.at[pl.ds(margin, 2 * cells + margin)]

    def get_rows(ref, first, count):
        return jnp.concatenate(
            [ref[pl.ds(2 * first + h, count, stride=2), :] for h in range(2)], axis=1
        )

    def put_rows(ref, first, count, value):
        for h in range(2):
            ref[pl.ds(2 * first + h, count, stride=2), :] = value[:, h * half : (h + 1) * half]

    side = 4
    last = tiles - 1

    def distance(k):
        return jnp.where(k == 0, 0, jnp.where(k == 1, 3, k - 1))

    def shifted(n, sign):
        y = lax.rem(tile // side + sign * distance(n // side) + side, side)
        x = lax.rem(lax.rem(tile, side) + sign * distance(lax.rem(n, side)) + side, side)
        return y * side + x

    load_chunks = 4
    chunk = cells // load_chunks

    def load(k):
        part = pl.ds(k * chunk, chunk)
        return pltpu.make_async_copy(state_ref.at[0, part], rows_bf.at[part], load_sem.at[k])

    small = [
        pltpu.make_async_copy(source, target, small_sem.at[q])
        for q, (source, target) in enumerate(
            (
                (couple_rows_hbm, couple_rows_ref),
                (couple_count_hbm, couple_count_ref),
                (cycle_hbm, cycle_ref),
                (halo_rows_hbm, halo_rows_ref),
                (halo_count_hbm, halo_count_ref),
                (couple_land_hbm, couple_land_ref),
                (couple_weight_hbm, couple_weight_ref),
                (dw_hbm, dw_ref),
                (gain_hbm, gain_ref),
                (up_hbm, up_ref),
                (bias_hbm, bias_ref),
                (down_hbm, down_ref),
            )
        )
    ]
    for k in range(load_chunks):
        load(k).start()
    barrier = pltpu.get_barrier_semaphore()

    def greet(n, carry):
        pl.semaphore_signal(
            barrier, inc=1, device_id=place(comp, face, shifted(n, 1)), device_id_type=MESH
        )
        return carry

    lax.fori_loop(1, tiles, greet, 0)
    for target in (place(other, face, tile), near[2], near[3]):
        pl.semaphore_signal(barrier, inc=1, device_id=target, device_id_type=MESH)
    for copy in small:
        copy.start()

    rows_all[pl.ds(0, margin), :] = jnp.zeros((margin, half), F32)
    rows_all[pl.ds(2 * cells + margin, margin), :] = jnp.zeros((margin, half), F32)
    for k in range(load_chunks):
        load(k).wait()

        def widen(i, carry, k=k):
            first = k * chunk + i * 256
            part = pl.ds(pl.multiple_of(first, 256), 256)
            put_rows(rows, first, 256, rows_bf[part, :].astype(F32))
            return carry

        lax.fori_loop(0, chunk // 256, widen, 0)

    for copy in small[:9]:
        copy.wait()
    pl.semaphore_wait(barrier, last + 3)

    def cycle_copy(d):
        return pltpu.make_async_remote_copy(
            src_ref=cycle_ref,
            dst_ref=cycle_near.at[d],
            send_sem=cycle_send_sem.at[d],
            recv_sem=cycle_recv_sem.at[d],
            device_id=near[d ^ 1],
            device_id_type=MESH,
        )

    for d in range(4):
        cycle_copy(d).start()

    def slot_rows(n):
        return pl.ds(pl.multiple_of(n * slots, slots), slots)

    def pass_copy(n):
        return pltpu.make_async_remote_copy(
            src_ref=send_rows.at[slot_rows(n)],
            dst_ref=via_rows.at[slot_rows(n)],
            send_sem=pass_send_sem.at[n],
            recv_sem=pass_recv_sem.at[n],
            device_id=place(comp, face, shifted(n, 1)),
            device_id_type=MESH,
        )

    def cross_copy(n):
        own = isinstance(n, int) and n == 0
        return pltpu.make_async_remote_copy(
            src_ref=(send_rows if own else via_rows).at[slot_rows(n)],
            dst_ref=recv_rows.at[slot_rows(n)],
            send_sem=cross_send_sem.at[n],
            recv_sem=cross_recv_sem.at[n],
            device_id=place(other, face, tile),
            device_id_type=MESH,
        )

    def gather(n):
        dest = shifted(n, 1)
        live = couple_count_ref[0, dest]
        step = slots

        def pick(g, inner):
            base = pl.multiple_of(g * step, step)
            index = [
                jnp.where(base + u < live, couple_rows_ref[0, dest, base + u], cells)
                for u in range(step)
            ]
            values = [rows[pl.ds(2 * i, 2), :] for i in index]
            for u in range(step):
                picked[pl.ds(pl.multiple_of(2 * base, 2 * step) + 2 * u, 2), :] = values[u]
            return inner

        lax.fori_loop(0, slots // step, pick, 0)
        send_rows[slot_rows(n), :] = get_rows(picked, 0, slots).astype(BF16)

    def gather_send(n, carry):
        gather(n)
        pass_copy(n).start()
        return carry

    gather(0)
    cross_copy(0).start()
    lax.fori_loop(1, tiles, gather_send, 0)

    for d in range(4):
        cycle_copy(d).wait()
    index_i32[...] = jnp.full(index_i32.shape, cells, jnp.int32)
    groups = rim_rows // 128
    sub = lax.broadcasted_iota(jnp.int32, (128, cycle_len), 0)
    for d in range(4):
        table = jnp.transpose(
            jnp.concatenate(
                [halo_rows_ref[0, d : d + 1, 128 * g : 128 * (g + 1)] for g in range(groups)], axis=0
            )
        )
        slot = cycle_near[d] - d * rim_rows
        group = jnp.right_shift(slot, 7)
        found = jnp.zeros((128, cycle_len), jnp.int32)
        for g in range(groups):
            found = jnp.where(group == g, table[:, g : g + 1], found)
        found = jnp.where(jnp.bitwise_and(slot, 127) == sub, found, 0)
        found = sum(found[8 * k : 8 * k + 8] for k in range(16))
        row = sum(found[k : k + 1] for k in range(8))
        live = (slot >= 0) & (slot < halo_count_ref[0, d])
        index_i32[d : d + 1, pl.ds(0, cycle_len)] = jnp.where(live, row, cells)
    to_smem = pltpu.make_async_copy(index_i32, index_smem, smem_sem)
    to_smem.start()
    turned = jnp.transpose(index_i32[...].astype(F32))
    for d in range(4):
        index_col[pl.ds(d * border_rows, border_rows), :] = jnp.broadcast_to(
            turned[:border_rows, d : d + 1], (border_rows, 128)
        )

    def forward(n, carry):
        pass_copy(n).wait_recv()
        cross_copy(n).start()
        return carry

    pair = 2 * slots
    pairs = tiles // 2
    early = pairs - 3
    lane_col = lax.broadcasted_iota(jnp.int32, (GRID_W, pair), 0)

    def project(p):
        part = pl.ds(pl.multiple_of(p * pair, pair), pair)
        value = jnp.dot(recv_rows[part, :], couple_weight_ref[0], preferred_element_type=F32)
        arrived[p] = value.astype(BF16)

    def land_lanes(p):
        return jnp.concatenate(
            [couple_land_ref[0, pl.ds(shifted(2 * p + q, -1), 1), :] for q in range(2)], axis=1
        )

    def landed(p):
        land = land_lanes(p)
        land_row = jnp.right_shift(land, 7)
        in_col = jnp.where(jnp.bitwise_and(land, GRID_W - 1) == lane_col, 1.0, 0.0).astype(BF16)
        hot = jnp.concatenate(
            [in_col * jnp.where(land_row == i, 1.0, 0.0).astype(BF16) for i in range(height)], axis=0
        )
        added = jnp.dot(hot, arrived[p], preferred_element_type=F32)
        return get_rows(rows, 0, cells) + added

    def land_pair(p):
        cross_copy(2 * p).wait_recv()
        cross_copy(2 * p + 1).wait_recv()
        project(p)
        put_rows(rows, 0, cells, landed(p))

    step = 92

    def pick_halo(d):
        def pick(g, carry):
            values = [
                rows[pl.ds(2 * index_smem[d, g * step + u], 2), :] for u in range(step)
            ]
            start = pl.multiple_of(2 * (d * border_rows + g * step), 2 * step)
            for u in range(step):
                halo_part[pl.ds(start + 2 * u, 2), :] = values[u]
            return carry

        lax.fori_loop(0, border_rows // step, pick, 0)

    def land_step(p, carry):
        land_pair(p)
        return carry

    def forward_step(p, carry):
        lax.fori_loop(1 + 5 * p, 6 + 5 * p, forward, 0)
        land_pair(p)
        return carry

    lax.fori_loop(0, 3, forward_step, 0)
    lax.fori_loop(3, early, land_step, 0)
    to_smem.wait()

    def pick_step(d, carry):
        pick_halo(d)
        return carry

    lax.fori_loop(0, 4, pick_step, 0)
    lax.fori_loop(early, pairs - 1, land_step, 0)
    cross_copy(last - 1).wait_recv()
    cross_copy(last).wait_recv()

    project(pairs - 1)

    def halo_copy(d):
        return pltpu.make_async_remote_copy(
            src_ref=halo_send.at[d],
            dst_ref=halo_recv.at[d],
            send_sem=halo_send_sem.at[d],
            recv_sem=halo_recv_sem.at[d],
            device_id=near[d],
            device_id_type=MESH,
        )

    late_land = jnp.concatenate([land_lanes(p) for p in range(early, pairs)], axis=1).astype(F32)
    late_rows = jnp.concatenate([arrived[p] for p in range(early, pairs)], axis=0)
    for d in (2, 0):
        wanted = index_col[pl.ds(d * border_rows, 2 * border_rows), :]
        hot = jnp.concatenate(
            [
                jnp.where(wanted == late_land[:, 128 * k : 128 * (k + 1)], 1.0, 0.0).astype(BF16)
                for k in range(late_land.shape[1] // 128)
            ],
            axis=1,
        )
        value = get_rows(halo_part, d * border_rows, 2 * border_rows) + jnp.dot(
            hot, late_rows, preferred_element_type=F32
        )
        for q in range(2):
            halo_send[d + q] = value[q * border_rows : (q + 1) * border_rows].astype(BF16)
            halo_copy(d + q).start()

    joined = landed(pairs - 1).astype(BF16)
    rows_bf[...] = joined
    put_rows(rows, 0, cells, joined.astype(F32))

    taps = [dw_ref[q] for q in range(9)]
    gain = gain_ref[...]

    def mix(above, here, below):
        left, mid, right = (
            taps[c] * above + taps[3 + c] * here + taps[6 + c] * below for c in range(3)
        )
        return mid + pltpu.roll(left, 1, 0) + pltpu.roll(right, GRID_W - 1, 0)

    def grid_row(i):
        return get_rows(rows, i * GRID_W, GRID_W)

    def near_row(first):
        return jnp.concatenate(
            [rows_all[pl.ds(margin + 2 * first + h, GRID_W, stride=2), :] for h in range(2)], axis=1
        )

    band = 8
    bands = height // band

    def interior(b, carry):
        for q in range(band):
            i = b * band + q
            mixed = None
            for r in range(3):
                line = jnp.clip(i + r - 1, 0, height - 1) * GRID_W
                for c in range(3):
                    term = taps[3 * r + c] * near_row(line + c - 1)
                    mixed = term if mixed is None else mixed + term
            part = pl.ds(pl.multiple_of(i * GRID_W, GRID_W), GRID_W)
            normed[part, :] = norm(mixed, gain).astype(BF16)
        return carry

    lax.fori_loop(0, bands, interior, 0)

    for copy in small[9:]:
        copy.wait()
    down = (0.5 * down_ref[0].astype(F32)).astype(BF16)

    def mlp(value):
        before = jnp.dot(value, up_ref[0], preferred_element_type=F32) + bias_ref[...]
        return jnp.dot(twice_gelu(before).astype(BF16), down, preferred_element_type=F32)

    def level(first, size):
        part = pl.ds(first, size)
        out[part, :] = (rows_bf[part, :].astype(F32) + mlp(normed[part, :])).astype(BF16)

    def store(k, first, size):
        part = pl.ds(first, size)
        return pltpu.make_async_copy(out.at[part], out_hbm.at[0, part], store_sem.at[k])

    outer = ((1, 0), (2, 1), (3, GRID_W - 2), (4, GRID_W - 1))

    for q, col in outer:
        for h in range(2):
            column = rows[pl.ds(2 * col + h, height, stride=2 * GRID_W), :]
            columns[q, pl.ds(1, height), pl.ds(h * half, half)] = column
    for d in range(4):
        halo_copy(d).wait_recv()

    border[...] = (halo_recv[0].astype(F32) + halo_recv[1].astype(F32)) + (
        halo_recv[2].astype(F32) + halo_recv[3].astype(F32)
    )
    wide = GRID_W + 2
    for q, col in outer:
        columns[q, pl.ds(0, 1), :] = border[pl.ds(1 + col, 1), :]
        columns[q, pl.ds(height + 1, 1), :] = border[pl.ds(wide + 1 + col, 1), :]
    for q, corner, side in ((0, 0, 2 * wide), (5, wide - 1, 2 * wide + height)):
        columns[q, pl.ds(0, 1), :] = border[pl.ds(corner, 1), :]
        columns[q, pl.ds(1, height), :] = border[pl.ds(side, height), :]
        columns[q, pl.ds(height + 1, 1), :] = border[pl.ds(wide + corner, 1), :]
    mixed = [
        mix(border[pl.ds(1, GRID_W), :], grid_row(0), grid_row(1)),
        mix(grid_row(height - 2), grid_row(height - 1), border[pl.ds(wide + 1, GRID_W), :]),
    ]
    for first in (0, 3):
        total = None
        for r in range(3):
            for c in range(3):
                term = taps[3 * r + c] * columns[first + c, pl.ds(r, height), :]
                total = term if total is None else total + term
        mixed.append(total)
    edges = norm(jnp.concatenate(mixed, axis=0), gain)
    line = lax.broadcasted_iota(jnp.int32, (TILE, channels), 0)

    def merge(ref, i, left, right):
        for fresh, first, at in ((left, 0, 0), (right, GRID_W - TILE, TILE - 1)):
            box = pl.ds(i * GRID_W + first, TILE)
            fixed = jnp.where(line == at, fresh, ref[box, :].astype(F32))
            ref[box, :] = fixed.astype(BF16)

    lefts, rights = 2 * GRID_W, 2 * GRID_W + height
    normed[pl.ds(cells - GRID_W, GRID_W), :] = edges[GRID_W : 2 * GRID_W].astype(BF16)
    normed[pl.ds(0, GRID_W), :] = edges[:GRID_W].astype(BF16)
    for i in range(height):
        merge(normed, i, edges[lefts + i : lefts + i + 1], edges[rights + i : rights + i + 1])
    block = 1024
    stores = []
    for first in range(0, cells, block):
        level(first, block)
        stores.append(store(len(stores), first, block))
        stores[-1].start()

    for n in range(tiles):
        cross_copy(n).wait_send()
    for n in range(1, tiles):
        pass_copy(n).wait_send()
    for d in range(4):
        halo_copy(d).wait_send()
    for copy in stores:
        copy.wait()


def twice_gelu(before):
    inner = before * (0.7978845608028654 + 0.035677408136300125 * (before * before))
    return before + before * jnp.tanh(inner)


def body(
    state,
    cycle_source,
    halo_rows,
    halo_count,
    couple_rows,
    couple_count,
    couple_land,
    couple_weight,
    dw_weight,
    norm_gain,
    up_weight,
    up_bias,
    down_weight,
):
    _, cells, channels = state.shape
    tiles, faces = lax.axis_size("tile"), lax.axis_size("face")
    cycle_len = cycle_source.shape[1]
    border_rows = -(-cycle_len // TILE) * TILE
    index_lanes = -(-cycle_len // 128) * 128
    slots = couple_rows.shape[2]
    height = cells // GRID_W
    hbm = pl.BlockSpec(memory_space=pl.ANY)
    dma = pltpu.SemaphoreType.DMA
    vmem = pltpu.VMEM
    return pl.pallas_call(
        functools.partial(couple_kernel, tiles, faces, cycle_len),
        name="couple_and_mix",
        out_shape=jax.ShapeDtypeStruct((1, cells, channels), BF16),
        in_specs=[hbm] * 13,
        out_specs=hbm,
        scratch_shapes=[
            vmem((1, cycle_len), jnp.int32),
            vmem(halo_rows.shape, jnp.int32),
            pltpu.SMEM((1, 4), jnp.int32),
            pltpu.SMEM(couple_rows.shape, jnp.int32),
            pltpu.SMEM((1, tiles), jnp.int32),
            vmem(couple_land.shape, jnp.int32),
            vmem(couple_weight.shape, BF16),
            vmem((9, 1, channels), F32),
            vmem((1, channels), F32),
            vmem(up_weight.shape, BF16),
            vmem(up_bias.shape, F32),
            vmem(down_weight.shape, BF16),
            vmem((cells, channels), BF16),
            vmem((2 * cells + 32, channels // 2), F32),
            vmem((2 * slots, channels // 2), F32),
            vmem((tiles * slots, channels), BF16),
            vmem((tiles * slots, channels), BF16),
            vmem((tiles * slots, channels), BF16),
            vmem((tiles // 2, 2 * slots, channels), BF16),
            vmem((4, 1, cycle_len), jnp.int32),
            vmem((8, index_lanes), jnp.int32),
            pltpu.SMEM((8, index_lanes), jnp.int32),
            vmem((4 * border_rows, 128), F32),
            vmem((4 * 2 * border_rows, channels // 2), F32),
            vmem((4, border_rows, channels), BF16),
            vmem((4, border_rows, channels), BF16),
            vmem((border_rows, channels), F32),
            vmem((6, height + 8, channels), F32),
            vmem((cells, channels), BF16),
            vmem((cells, channels), BF16),
            dma((4,)),
            dma((12,)),
            dma,
            dma((6,)),
            dma((tiles,)),
            dma((tiles,)),
            dma((tiles,)),
            dma((tiles,)),
            dma((4,)),
            dma((4,)),
            dma((4,)),
            dma((4,)),
        ],
        compiler_params=pltpu.CompilerParams(
            collective_id=0, has_side_effects=True, vmem_limit_bytes=64 << 20
        ),
    )(
        state,
        cycle_source,
        halo_rows,
        halo_count.reshape(1, 4),
        couple_rows,
        couple_count.reshape(1, tiles),
        couple_land,
        couple_weight,
        jnp.transpose(dw_weight, (1, 0, 2)),
        norm_gain,
        up_weight,
        up_bias,
        down_weight,
    )


def solution(mesh):
    in_specs = (
        P("comp", ("face", "tile"), None),
        P("comp", ("face", "tile")),
        P("comp", None, ("face", "tile")),
        P("comp", None, ("face", "tile")),
        P("comp", None, ("face", "tile")),
        P("comp", None, ("face", "tile")),
        P("comp", None, ("face", "tile")),
        P("comp", None, None),
        P("comp", None, None),
        P("comp", None),
        P("comp", None, None),
        P("comp", None),
        P("comp", None, None),
    )
    out_specs = P("comp", ("face", "tile"), None)
    return jax.shard_map(body, mesh=mesh, in_specs=in_specs, out_specs=out_specs, check_vma=False)
```

```python
import functools

import jax
import jax.numpy as jnp
from jax import lax
from jax.experimental import pallas as pl
from jax.experimental.pallas import tpu as pltpu
from jax.sharding import PartitionSpec as P

MESH = pl.DeviceIdType.MESH
GRID_W = 128
F32 = jnp.float32
BF16 = jnp.bfloat16
TILE = 16


def place(comp, face, tile):
    return {"comp": comp, "face": face, "tile": tile}


def norm(mixed, gain):
    center = mixed - jnp.mean(mixed, axis=-1, keepdims=True)
    spread = jnp.mean(center * center, axis=-1, keepdims=True)
    return center * lax.rsqrt(spread + 1e-06) * gain


def couple_kernel(
    tiles,
    faces,
    cycle_len,
    state_ref,
    cycle_hbm,
    halo_rows_hbm,
    halo_count_hbm,
    couple_rows_hbm,
    couple_count_hbm,
    couple_land_hbm,
    couple_weight_hbm,
    dw_hbm,
    gain_hbm,
    up_hbm,
    bias_hbm,
    down_hbm,
    out_hbm,
    cycle_ref,
    halo_rows_ref,
    halo_count_ref,
    couple_rows_ref,
    couple_count_ref,
    couple_land_ref,
    couple_weight_ref,
    dw_ref,
    gain_ref,
    up_ref,
    bias_ref,
    down_ref,
    rows_bf,
    rows_all,
    picked,
    send_rows,
    via_rows,
    recv_rows,
    arrived,
    cycle_near,
    index_i32,
    index_smem,
    index_col,
    halo_part,
    halo_send,
    halo_recv,
    border,
    columns,
    normed,
    out,
    load_sem,
    small_sem,
    smem_sem,
    store_sem,
    cross_send_sem,
    cross_recv_sem,
    pass_send_sem,
    pass_recv_sem,
    cycle_send_sem,
    cycle_recv_sem,
    halo_send_sem,
    halo_recv_sem,
):
    comp, face, tile = lax.axis_index("comp"), lax.axis_index("face"), lax.axis_index("tile")
    cells, channels = rows_bf.shape
    half = channels // 2
    height = cells // GRID_W
    slots = couple_rows_ref.shape[2]
    rim_rows = halo_rows_ref.shape[2]
    border_rows = halo_send.shape[1]
    other = 1 - comp
    near = [
        place(comp, face, lax.rem(tile + 1, tiles)),
        place(comp, face, lax.rem(tile + tiles - 1, tiles)),
        place(comp, lax.rem(face + 1, faces), tile),
        place(comp, lax.rem(face + faces - 1, faces), tile),
    ]

    margin = 16
    rows = rows_all.at[pl.ds(margin, 2 * cells + margin)]

    def get_rows(ref, first, count):
        return jnp.concatenate(
            [ref[pl.ds(2 * first + h, count, stride=2), :] for h in range(2)], axis=1
        )

    def put_rows(ref, first, count, value):
        for h in range(2):
            ref[pl.ds(2 * first + h, count, stride=2), :] = value[:, h * half : (h + 1) * half]

    side = 4
    last = tiles - 1

    def distance(k):
        return jnp.where(k == 0, 0, jnp.where(k == 1, 3, k - 1))

    def shifted(n, sign):
        y = lax.rem(tile // side + sign * distance(n // side) + side, side)
        x = lax.rem(lax.rem(tile, side) + sign * distance(lax.rem(n, side)) + side, side)
        return y * side + x

    load_chunks = 4
    chunk = cells // load_chunks

    def load(k):
        part = pl.ds(k * chunk, chunk)
        return pltpu.make_async_copy(state_ref.at[0, part], rows_bf.at[part], load_sem.at[k])

    small = [
        pltpu.make_async_copy(source, target, small_sem.at[q])
        for q, (source, target) in enumerate(
            (
                (couple_rows_hbm, couple_rows_ref),
                (couple_count_hbm, couple_count_ref),
                (cycle_hbm, cycle_ref),
                (halo_rows_hbm, halo_rows_ref),
                (halo_count_hbm, halo_count_ref),
                (couple_land_hbm, couple_land_ref),
                (couple_weight_hbm, couple_weight_ref),
                (dw_hbm, dw_ref),
                (gain_hbm, gain_ref),
                (up_hbm, up_ref),
                (bias_hbm, bias_ref),
                (down_hbm, down_ref),
            )
        )
    ]
    for k in range(load_chunks):
        load(k).start()
    barrier = pltpu.get_barrier_semaphore()

    def greet(n, carry):
        pl.semaphore_signal(
            barrier, inc=1, device_id=place(comp, face, shifted(n, 1)), device_id_type=MESH
        )
        return carry

    lax.fori_loop(1, tiles, greet, 0)
    for target in (place(other, face, tile), near[2], near[3]):
        pl.semaphore_signal(barrier, inc=1, device_id=target, device_id_type=MESH)
    for copy in small:
        copy.start()

    rows_all[pl.ds(0, margin), :] = jnp.zeros((margin, half), F32)
    rows_all[pl.ds(2 * cells + margin, margin), :] = jnp.zeros((margin, half), F32)
    for k in range(load_chunks):
        load(k).wait()

        def widen(i, carry, k=k):
            first = k * chunk + i * 256
            part = pl.ds(pl.multiple_of(first, 256), 256)
            put_rows(rows, first, 256, rows_bf[part, :].astype(F32))
            return carry

        lax.fori_loop(0, chunk // 256, widen, 0)

    for copy in small[:9]:
        copy.wait()
    pl.semaphore_wait(barrier, last + 3)

    def cycle_copy(d):
        return pltpu.make_async_remote_copy(
            src_ref=cycle_ref,
            dst_ref=cycle_near.at[d],
            send_sem=cycle_send_sem.at[d],
            recv_sem=cycle_recv_sem.at[d],
            device_id=near[d ^ 1],
            device_id_type=MESH,
        )

    for d in range(4):
        cycle_copy(d).start()

    def slot_rows(n):
        return pl.ds(pl.multiple_of(n * slots, slots), slots)

    def pass_copy(n):
        return pltpu.make_async_remote_copy(
            src_ref=send_rows.at[slot_rows(n)],
            dst_ref=via_rows.at[slot_rows(n)],
            send_sem=pass_send_sem.at[n],
            recv_sem=pass_recv_sem.at[n],
            device_id=place(comp, face, shifted(n, 1)),
            device_id_type=MESH,
        )

    def cross_copy(n):
        own = isinstance(n, int) and n == 0
        return pltpu.make_async_remote_copy(
            src_ref=(send_rows if own else via_rows).at[slot_rows(n)],
            dst_ref=recv_rows.at[slot_rows(n)],
            send_sem=cross_send_sem.at[n],
            recv_sem=cross_recv_sem.at[n],
            device_id=place(other, face, tile),
            device_id_type=MESH,
        )

    def gather(n):
        dest = shifted(n, 1)
        live = couple_count_ref[0, dest]
        step = slots

        def pick(g, inner):
            base = pl.multiple_of(g * step, step)
            index = [
                jnp.where(base + u < live, couple_rows_ref[0, dest, base + u], cells)
                for u in range(step)
            ]
            values = [rows[pl.ds(2 * i, 2), :] for i in index]
            for u in range(step):
                picked[pl.ds(pl.multiple_of(2 * base, 2 * step) + 2 * u, 2), :] = values[u]
            return inner

        lax.fori_loop(0, slots // step, pick, 0)
        send_rows[slot_rows(n), :] = get_rows(picked, 0, slots).astype(BF16)

    def gather_send(n, carry):
        gather(n)
        pass_copy(n).start()
        return carry

    def forward(n, carry):
        pass_copy(n).wait_recv()
        cross_copy(n).start()
        return carry

    first_batch = 3
    gather(0)
    cross_copy(0).start()
    lax.fori_loop(1, tiles, gather_send, 0)
    lax.fori_loop(1, 1 + first_batch, forward, 0)

    for d in range(4):
        cycle_copy(d).wait()
    index_i32[...] = jnp.full(index_i32.shape, cells, jnp.int32)
    groups = rim_rows // 128
    sub = lax.broadcasted_iota(jnp.int32, (128, cycle_len), 0)
    for d in range(4):
        table = jnp.transpose(
            jnp.concatenate(
                [halo_rows_ref[0, d : d + 1, 128 * g : 128 * (g + 1)] for g in range(groups)], axis=0
            )
        )
        slot = cycle_near[d] - d * rim_rows
        group = jnp.right_shift(slot, 7)
        found = jnp.zeros((128, cycle_len), jnp.int32)
        for g in range(groups):
            found = jnp.where(group == g, table[:, g : g + 1], found)
        found = jnp.where(jnp.bitwise_and(slot, 127) == sub, found, 0)
        found = sum(found[8 * k : 8 * k + 8] for k in range(16))
        row = sum(found[k : k + 1] for k in range(8))
        live = (slot >= 0) & (slot < halo_count_ref[0, d])
        index_i32[d : d + 1, pl.ds(0, cycle_len)] = jnp.where(live, row, cells)
    to_smem = pltpu.make_async_copy(index_i32, index_smem, smem_sem)
    to_smem.start()
    turned = jnp.transpose(index_i32[...].astype(F32))
    for d in range(4):
        index_col[pl.ds(d * border_rows, border_rows), :] = jnp.broadcast_to(
            turned[:border_rows, d : d + 1], (border_rows, 128)
        )

    pair = 2 * slots
    pairs = tiles // 2
    early = pairs - 3
    lane_col = lax.broadcasted_iota(jnp.int32, (GRID_W, pair), 0)

    def project(p):
        part = pl.ds(pl.multiple_of(p * pair, pair), pair)
        value = jnp.dot(recv_rows[part, :], couple_weight_ref[0], preferred_element_type=F32)
        arrived[p] = value.astype(BF16)

    def land_lanes(p):
        return jnp.concatenate(
            [couple_land_ref[0, pl.ds(shifted(2 * p + q, -1), 1), :] for q in range(2)], axis=1
        )

    def landed(p):
        land = land_lanes(p)
        land_row = jnp.right_shift(land, 7)
        in_col = jnp.where(jnp.bitwise_and(land, GRID_W - 1) == lane_col, 1.0, 0.0).astype(BF16)
        hot = jnp.concatenate(
            [in_col * jnp.where(land_row == i, 1.0, 0.0).astype(BF16) for i in range(height)], axis=0
        )
        added = jnp.dot(hot, arrived[p], preferred_element_type=F32)
        return get_rows(rows, 0, cells) + added

    def land_pair(p):
        cross_copy(2 * p).wait_recv()
        cross_copy(2 * p + 1).wait_recv()
        project(p)
        put_rows(rows, 0, cells, landed(p))

    step = 92

    def pick_halo(d):
        def pick(g, carry):
            values = [
                rows[pl.ds(2 * index_smem[d, g * step + u], 2), :] for u in range(step)
            ]
            start = pl.multiple_of(2 * (d * border_rows + g * step), 2 * step)
            for u in range(step):
                halo_part[pl.ds(start + 2 * u, 2), :] = values[u]
            return carry

        lax.fori_loop(0, border_rows // step, pick, 0)

    def land_step(p, carry):
        land_pair(p)
        return carry

    def forward_step(p, carry):
        rest = 1 + first_batch + 4 * p
        lax.fori_loop(rest, rest + 4, forward, 0)
        land_pair(p)
        return carry

    lax.fori_loop(0, 3, forward_step, 0)
    lax.fori_loop(3, early, land_step, 0)
    to_smem.wait()

    def pick_step(d, carry):
        pick_halo(d)
        return carry

    lax.fori_loop(0, 4, pick_step, 0)
    lax.fori_loop(early, pairs - 1, land_step, 0)
    cross_copy(last - 1).wait_recv()
    cross_copy(last).wait_recv()

    project(pairs - 1)

    def halo_copy(d):
        return pltpu.make_async_remote_copy(
            src_ref=halo_send.at[d],
            dst_ref=halo_recv.at[d],
            send_sem=halo_send_sem.at[d],
            recv_sem=halo_recv_sem.at[d],
            device_id=near[d],
            device_id_type=MESH,
        )

    late_land = jnp.concatenate([land_lanes(p) for p in range(early, pairs)], axis=1).astype(F32)
    late_rows = jnp.concatenate([arrived[p] for p in range(early, pairs)], axis=0)
    for d in (2, 0):
        wanted = index_col[pl.ds(d * border_rows, 2 * border_rows), :]
        hot = jnp.concatenate(
            [
                jnp.where(wanted == late_land[:, 128 * k : 128 * (k + 1)], 1.0, 0.0).astype(BF16)
                for k in range(late_land.shape[1] // 128)
            ],
            axis=1,
        )
        value = get_rows(halo_part, d * border_rows, 2 * border_rows) + jnp.dot(
            hot, late_rows, preferred_element_type=F32
        )
        for q in range(2):
            halo_send[d + q] = value[q * border_rows : (q + 1) * border_rows].astype(BF16)
            halo_copy(d + q).start()

    joined = landed(pairs - 1).astype(BF16)
    rows_bf[...] = joined
    put_rows(rows, 0, cells, joined.astype(F32))

    taps = [dw_ref[q] for q in range(9)]
    gain = gain_ref[...]

    def mix(above, here, below):
        left, mid, right = (
            taps[c] * above + taps[3 + c] * here + taps[6 + c] * below for c in range(3)
        )
        return mid + pltpu.roll(left, 1, 0) + pltpu.roll(right, GRID_W - 1, 0)

    def grid_row(i):
        return get_rows(rows, i * GRID_W, GRID_W)

    def near_row(first):
        return jnp.concatenate(
            [rows_all[pl.ds(margin + 2 * first + h, GRID_W, stride=2), :] for h in range(2)], axis=1
        )

    band = 8
    bands = height // band

    def interior(b, carry):
        for q in range(band):
            i = b * band + q
            mixed = None
            for r in range(3):
                line = jnp.clip(i + r - 1, 0, height - 1) * GRID_W
                for c in range(3):
                    term = taps[3 * r + c] * near_row(line + c - 1)
                    mixed = term if mixed is None else mixed + term
            part = pl.ds(pl.multiple_of(i * GRID_W, GRID_W), GRID_W)
            normed[part, :] = norm(mixed, gain).astype(BF16)
        return carry

    lax.fori_loop(0, bands, interior, 0)

    for copy in small[9:]:
        copy.wait()
    down = (0.5 * down_ref[0].astype(F32)).astype(BF16)

    def mlp(value):
        before = jnp.dot(value, up_ref[0], preferred_element_type=F32) + bias_ref[...]
        return jnp.dot(twice_gelu(before).astype(BF16), down, preferred_element_type=F32)

    def level(first, size):
        part = pl.ds(first, size)
        out[part, :] = (rows_bf[part, :].astype(F32) + mlp(normed[part, :])).astype(BF16)

    def store(k, first, size):
        part = pl.ds(first, size)
        return pltpu.make_async_copy(out.at[part], out_hbm.at[0, part], store_sem.at[k])

    outer = ((1, 0), (2, 1), (3, GRID_W - 2), (4, GRID_W - 1))

    for q, col in outer:
        for h in range(2):
            column = rows[pl.ds(2 * col + h, height, stride=2 * GRID_W), :]
            columns[q, pl.ds(1, height), pl.ds(h * half, half)] = column
    for d in range(4):
        halo_copy(d).wait_recv()

    border[...] = (halo_recv[0].astype(F32) + halo_recv[1].astype(F32)) + (
        halo_recv[2].astype(F32) + halo_recv[3].astype(F32)
    )
    wide = GRID_W + 2
    for q, col in outer:
        columns[q, pl.ds(0, 1), :] = border[pl.ds(1 + col, 1), :]
        columns[q, pl.ds(height + 1, 1), :] = border[pl.ds(wide + 1 + col, 1), :]
    for q, corner, side in ((0, 0, 2 * wide), (5, wide - 1, 2 * wide + height)):
        columns[q, pl.ds(0, 1), :] = border[pl.ds(corner, 1), :]
        columns[q, pl.ds(1, height), :] = border[pl.ds(side, height), :]
        columns[q, pl.ds(height + 1, 1), :] = border[pl.ds(wide + corner, 1), :]
    mixed = [
        mix(border[pl.ds(1, GRID_W), :], grid_row(0), grid_row(1)),
        mix(grid_row(height - 2), grid_row(height - 1), border[pl.ds(wide + 1, GRID_W), :]),
    ]
    for first in (0, 3):
        total = None
        for r in range(3):
            for c in range(3):
                term = taps[3 * r + c] * columns[first + c, pl.ds(r, height), :]
                total = term if total is None else total + term
        mixed.append(total)
    edges = norm(jnp.concatenate(mixed, axis=0), gain)
    line = lax.broadcasted_iota(jnp.int32, (TILE, channels), 0)

    def merge(ref, i, left, right):
        for fresh, first, at in ((left, 0, 0), (right, GRID_W - TILE, TILE - 1)):
            box = pl.ds(i * GRID_W + first, TILE)
            fixed = jnp.where(line == at, fresh, ref[box, :].astype(F32))
            ref[box, :] = fixed.astype(BF16)

    lefts, rights = 2 * GRID_W, 2 * GRID_W + height
    normed[pl.ds(cells - GRID_W, GRID_W), :] = edges[GRID_W : 2 * GRID_W].astype(BF16)
    normed[pl.ds(0, GRID_W), :] = edges[:GRID_W].astype(BF16)
    for i in range(height):
        merge(normed, i, edges[lefts + i : lefts + i + 1], edges[rights + i : rights + i + 1])
    block = 1024
    stores = []
    for first in range(0, cells, block):
        level(first, block)
        stores.append(store(len(stores), first, block))
        stores[-1].start()

    for n in range(tiles):
        cross_copy(n).wait_send()
    for n in range(1, tiles):
        pass_copy(n).wait_send()
    for d in range(4):
        halo_copy(d).wait_send()
    for copy in stores:
        copy.wait()


def twice_gelu(before):
    inner = before * (0.7978845608028654 + 0.035677408136300125 * (before * before))
    return before + before * jnp.tanh(inner)


def body(
    state,
    cycle_source,
    halo_rows,
    halo_count,
    couple_rows,
    couple_count,
    couple_land,
    couple_weight,
    dw_weight,
    norm_gain,
    up_weight,
    up_bias,
    down_weight,
):
    _, cells, channels = state.shape
    tiles, faces = lax.axis_size("tile"), lax.axis_size("face")
    cycle_len = cycle_source.shape[1]
    border_rows = -(-cycle_len // TILE) * TILE
    index_lanes = -(-cycle_len // 128) * 128
    slots = couple_rows.shape[2]
    height = cells // GRID_W
    hbm = pl.BlockSpec(memory_space=pl.ANY)
    dma = pltpu.SemaphoreType.DMA
    vmem = pltpu.VMEM
    return pl.pallas_call(
        functools.partial(couple_kernel, tiles, faces, cycle_len),
        name="couple_and_mix",
        out_shape=jax.ShapeDtypeStruct((1, cells, channels), BF16),
        in_specs=[hbm] * 13,
        out_specs=hbm,
        scratch_shapes=[
            vmem((1, cycle_len), jnp.int32),
            vmem(halo_rows.shape, jnp.int32),
            pltpu.SMEM((1, 4), jnp.int32),
            pltpu.SMEM(couple_rows.shape, jnp.int32),
            pltpu.SMEM((1, tiles), jnp.int32),
            vmem(couple_land.shape, jnp.int32),
            vmem(couple_weight.shape, BF16),
            vmem((9, 1, channels), F32),
            vmem((1, channels), F32),
            vmem(up_weight.shape, BF16),
            vmem(up_bias.shape, F32),
            vmem(down_weight.shape, BF16),
            vmem((cells, channels), BF16),
            vmem((2 * cells + 32, channels // 2), F32),
            vmem((2 * slots, channels // 2), F32),
            vmem((tiles * slots, channels), BF16),
            vmem((tiles * slots, channels), BF16),
            vmem((tiles * slots, channels), BF16),
            vmem((tiles // 2, 2 * slots, channels), BF16),
            vmem((4, 1, cycle_len), jnp.int32),
            vmem((8, index_lanes), jnp.int32),
            pltpu.SMEM((8, index_lanes), jnp.int32),
            vmem((4 * border_rows, 128), F32),
            vmem((4 * 2 * border_rows, channels // 2), F32),
            vmem((4, border_rows, channels), BF16),
            vmem((4, border_rows, channels), BF16),
            vmem((border_rows, channels), F32),
            vmem((6, height + 8, channels), F32),
            vmem((cells, channels), BF16),
            vmem((cells, channels), BF16),
            dma((4,)),
            dma((12,)),
            dma,
            dma((6,)),
            dma((tiles,)),
            dma((tiles,)),
            dma((tiles,)),
            dma((tiles,)),
            dma((4,)),
            dma((4,)),
            dma((4,)),
            dma((4,)),
        ],
        compiler_params=pltpu.CompilerParams(
            collective_id=0, has_side_effects=True, vmem_limit_bytes=64 << 20
        ),
    )(
        state,
        cycle_source,
        halo_rows,
        halo_count.reshape(1, 4),
        couple_rows,
        couple_count.reshape(1, tiles),
        couple_land,
        couple_weight,
        jnp.transpose(dw_weight, (1, 0, 2)),
        norm_gain,
        up_weight,
        up_bias,
        down_weight,
    )


def solution(mesh):
    in_specs = (
        P("comp", ("face", "tile"), None),
        P("comp", ("face", "tile")),
        P("comp", None, ("face", "tile")),
        P("comp", None, ("face", "tile")),
        P("comp", None, ("face", "tile")),
        P("comp", None, ("face", "tile")),
        P("comp", None, ("face", "tile")),
        P("comp", None, None),
        P("comp", None, None),
        P("comp", None),
        P("comp", None, None),
        P("comp", None),
        P("comp", None, None),
    )
    out_specs = P("comp", ("face", "tile"), None)
    return jax.shard_map(body, mesh=mesh, in_specs=in_specs, out_specs=out_specs, check_vma=False)
```

```python
import functools

import jax
import jax.numpy as jnp
from jax import lax
from jax.experimental import pallas as pl
from jax.experimental.pallas import tpu as pltpu
from jax.sharding import PartitionSpec as P

MESH = pl.DeviceIdType.MESH
GRID_W = 128
F32 = jnp.float32
BF16 = jnp.bfloat16
TILE = 16


def place(comp, face, tile):
    return {"comp": comp, "face": face, "tile": tile}


def norm(mixed, gain):
    center = mixed - jnp.mean(mixed, axis=-1, keepdims=True)
    spread = jnp.mean(center * center, axis=-1, keepdims=True)
    return center * lax.rsqrt(spread + 1e-06) * gain


def couple_kernel(
    tiles,
    faces,
    cycle_len,
    state_ref,
    cycle_hbm,
    halo_rows_hbm,
    halo_count_hbm,
    couple_rows_hbm,
    couple_count_hbm,
    couple_land_hbm,
    couple_weight_hbm,
    dw_hbm,
    gain_hbm,
    up_hbm,
    bias_hbm,
    down_hbm,
    out_hbm,
    cycle_ref,
    halo_rows_ref,
    halo_count_ref,
    couple_rows_ref,
    couple_count_ref,
    couple_land_ref,
    couple_weight_ref,
    dw_ref,
    gain_ref,
    up_ref,
    bias_ref,
    down_ref,
    rows_bf,
    rows_all,
    picked,
    send_rows,
    via_rows,
    recv_rows,
    arrived,
    cycle_near,
    index_i32,
    index_smem,
    index_col,
    halo_part,
    halo_send,
    halo_recv,
    border,
    columns,
    normed,
    out,
    load_sem,
    small_sem,
    smem_sem,
    store_sem,
    cross_send_sem,
    cross_recv_sem,
    pass_send_sem,
    pass_recv_sem,
    cycle_send_sem,
    cycle_recv_sem,
    halo_send_sem,
    halo_recv_sem,
):
    comp, face, tile = lax.axis_index("comp"), lax.axis_index("face"), lax.axis_index("tile")
    cells, channels = rows_bf.shape
    half = channels // 2
    height = cells // GRID_W
    slots = couple_rows_ref.shape[2]
    rim_rows = halo_rows_ref.shape[2]
    border_rows = halo_send.shape[1]
    other = 1 - comp
    near = [
        place(comp, face, lax.rem(tile + 1, tiles)),
        place(comp, face, lax.rem(tile + tiles - 1, tiles)),
        place(comp, lax.rem(face + 1, faces), tile),
        place(comp, lax.rem(face + faces - 1, faces), tile),
    ]

    margin = 16
    rows = rows_all.at[pl.ds(margin, 2 * cells + margin + 256)]

    def get_rows(ref, first, count):
        return jnp.concatenate(
            [ref[pl.ds(2 * first + h, count, stride=2), :] for h in range(2)], axis=1
        )

    def put_rows(ref, first, count, value):
        for h in range(2):
            ref[pl.ds(2 * first + h, count, stride=2), :] = value[:, h * half : (h + 1) * half]

    side = 4
    last = tiles - 1

    def distance(k):
        return jnp.where(k == 0, 0, jnp.where(k == 1, 3, k - 1))

    def shifted(n, sign):
        y = lax.rem(tile // side + sign * distance(n // side) + side, side)
        x = lax.rem(lax.rem(tile, side) + sign * distance(lax.rem(n, side)) + side, side)
        return y * side + x

    load_chunks = 4
    chunk = cells // load_chunks

    def load(k):
        part = pl.ds(k * chunk, chunk)
        return pltpu.make_async_copy(state_ref.at[0, part], rows_bf.at[part], load_sem.at[k])

    small = [
        pltpu.make_async_copy(source, target, small_sem.at[q])
        for q, (source, target) in enumerate(
            (
                (couple_rows_hbm, couple_rows_ref),
                (couple_count_hbm, couple_count_ref),
                (cycle_hbm, cycle_ref),
                (halo_rows_hbm, halo_rows_ref),
                (halo_count_hbm, halo_count_ref),
                (couple_land_hbm, couple_land_ref),
                (couple_weight_hbm, couple_weight_ref),
                (dw_hbm, dw_ref),
                (gain_hbm, gain_ref),
                (up_hbm, up_ref),
                (bias_hbm, bias_ref),
                (down_hbm, down_ref),
            )
        )
    ]
    for k in range(load_chunks):
        load(k).start()
    barrier = pltpu.get_barrier_semaphore()

    def greet(n, carry):
        pl.semaphore_signal(
            barrier, inc=1, device_id=place(comp, face, shifted(n, 1)), device_id_type=MESH
        )
        return carry

    lax.fori_loop(1, tiles, greet, 0)
    for target in (place(other, face, tile), near[2], near[3]):
        pl.semaphore_signal(barrier, inc=1, device_id=target, device_id_type=MESH)
    for copy in small:
        copy.start()

    rows_all[pl.ds(0, margin), :] = jnp.zeros((margin, half), F32)
    rows_all[pl.ds(2 * cells + margin, margin), :] = jnp.zeros((margin, half), F32)
    for k in range(load_chunks):
        load(k).wait()

        def widen(i, carry, k=k):
            first = k * chunk + i * 256
            part = pl.ds(pl.multiple_of(first, 256), 256)
            put_rows(rows, first, 256, rows_bf[part, :].astype(F32))
            return carry

        lax.fori_loop(0, chunk // 256, widen, 0)

    for copy in small[:9]:
        copy.wait()
    pl.semaphore_wait(barrier, last + 3)

    def cycle_copy(d):
        return pltpu.make_async_remote_copy(
            src_ref=cycle_ref,
            dst_ref=cycle_near.at[d],
            send_sem=cycle_send_sem.at[d],
            recv_sem=cycle_recv_sem.at[d],
            device_id=near[d ^ 1],
            device_id_type=MESH,
        )

    for d in range(4):
        cycle_copy(d).start()

    def slot_rows(n):
        return pl.ds(pl.multiple_of(n * slots, slots), slots)

    def pass_copy(n):
        return pltpu.make_async_remote_copy(
            src_ref=send_rows.at[slot_rows(n)],
            dst_ref=via_rows.at[slot_rows(n)],
            send_sem=pass_send_sem.at[n],
            recv_sem=pass_recv_sem.at[n],
            device_id=place(comp, face, shifted(n, 1)),
            device_id_type=MESH,
        )

    def cross_copy(n):
        own = isinstance(n, int) and n == 0
        return pltpu.make_async_remote_copy(
            src_ref=(send_rows if own else via_rows).at[slot_rows(n)],
            dst_ref=recv_rows.at[slot_rows(n)],
            send_sem=cross_send_sem.at[n],
            recv_sem=cross_recv_sem.at[n],
            device_id=place(other, face, tile),
            device_id_type=MESH,
        )

    def gather(n):
        dest = shifted(n, 1)
        live = couple_count_ref[0, dest]
        step = slots

        def pick(g, inner):
            base = pl.multiple_of(g * step, step)
            index = [
                jnp.where(base + u < live, couple_rows_ref[0, dest, base + u], cells)
                for u in range(step)
            ]
            values = [rows[pl.ds(2 * i, 2), :] for i in index]
            for u in range(step):
                picked[pl.ds(pl.multiple_of(2 * base, 2 * step) + 2 * u, 2), :] = values[u]
            return inner

        lax.fori_loop(0, slots // step, pick, 0)
        send_rows[slot_rows(n), :] = get_rows(picked, 0, slots).astype(BF16)

    def gather_send(n, carry):
        gather(n)
        pass_copy(n).start()
        return carry

    def forward(n, carry):
        pass_copy(n).wait_recv()
        cross_copy(n).start()
        return carry

    first_batch = 3
    gather(0)
    cross_copy(0).start()
    lax.fori_loop(1, tiles, gather_send, 0)
    lax.fori_loop(1, 1 + first_batch, forward, 0)

    for d in range(4):
        cycle_copy(d).wait()
    index_i32[...] = jnp.full(index_i32.shape, cells, jnp.int32)
    groups = rim_rows // 128
    sub = lax.broadcasted_iota(jnp.int32, (128, cycle_len), 0)
    for d in range(4):
        table = jnp.transpose(
            jnp.concatenate(
                [halo_rows_ref[0, d : d + 1, 128 * g : 128 * (g + 1)] for g in range(groups)], axis=0
            )
        )
        slot = cycle_near[d] - d * rim_rows
        group = jnp.right_shift(slot, 7)
        found = jnp.zeros((128, cycle_len), jnp.int32)
        for g in range(groups):
            found = jnp.where(group == g, table[:, g : g + 1], found)
        found = jnp.where(jnp.bitwise_and(slot, 127) == sub, found, 0)
        found = sum(found[8 * k : 8 * k + 8] for k in range(16))
        row = sum(found[k : k + 1] for k in range(8))
        live = (slot >= 0) & (slot < halo_count_ref[0, d])
        index_i32[d : d + 1, pl.ds(0, cycle_len)] = jnp.where(live, row, cells)
    to_smem = pltpu.make_async_copy(index_i32, index_smem, smem_sem)
    to_smem.start()
    turned = jnp.transpose(index_i32[...].astype(F32))
    for d in range(4):
        index_col[pl.ds(d * border_rows, border_rows), :] = jnp.broadcast_to(
            turned[:border_rows, d : d + 1], (border_rows, 128)
        )

    pair = 2 * slots
    pairs = tiles // 2
    early = pairs - 3
    lane_col = lax.broadcasted_iota(jnp.int32, (GRID_W, pair), 0)

    def project(p):
        part = pl.ds(pl.multiple_of(p * pair, pair), pair)
        value = jnp.dot(recv_rows[part, :], couple_weight_ref[0], preferred_element_type=F32)
        arrived[p] = value.astype(BF16)

    def land_lanes(p):
        return jnp.concatenate(
            [couple_land_ref[0, pl.ds(shifted(2 * p + q, -1), 1), :] for q in range(2)], axis=1
        )

    def landed(p):
        land = land_lanes(p)
        land_row = jnp.right_shift(land, 7)
        in_col = jnp.where(jnp.bitwise_and(land, GRID_W - 1) == lane_col, 1.0, 0.0).astype(BF16)
        hot = jnp.concatenate(
            [in_col * jnp.where(land_row == i, 1.0, 0.0).astype(BF16) for i in range(height)], axis=0
        )
        added = jnp.dot(hot, arrived[p], preferred_element_type=F32)
        return get_rows(rows, 0, cells) + added

    def land_pair(p):
        cross_copy(2 * p).wait_recv()
        cross_copy(2 * p + 1).wait_recv()
        project(p)
        put_rows(rows, 0, cells, landed(p))

    step = 92

    def pick_halo(d):
        def pick(g, carry):
            values = [
                rows[pl.ds(2 * index_smem[d, g * step + u], 2), :] for u in range(step)
            ]
            start = pl.multiple_of(2 * (d * border_rows + g * step), 2 * step)
            for u in range(step):
                halo_part[pl.ds(start + 2 * u, 2), :] = values[u]
            return carry

        lax.fori_loop(0, border_rows // step, pick, 0)

    def land_step(p, carry):
        land_pair(p)
        return carry

    def forward_step(p, carry):
        rest = 1 + first_batch + 4 * p
        lax.fori_loop(rest, rest + 4, forward, 0)
        land_pair(p)
        return carry

    lax.fori_loop(0, 3, forward_step, 0)
    lax.fori_loop(3, early, land_step, 0)
    to_smem.wait()

    def pick_step(d, carry):
        pick_halo(d)
        return carry

    lax.fori_loop(0, 4, pick_step, 0)
    lax.fori_loop(early, pairs - 1, land_step, 0)
    cross_copy(last - 1).wait_recv()
    cross_copy(last).wait_recv()

    project(pairs - 1)

    def halo_copy(d):
        return pltpu.make_async_remote_copy(
            src_ref=halo_send.at[d],
            dst_ref=halo_recv.at[d],
            send_sem=halo_send_sem.at[d],
            recv_sem=halo_recv_sem.at[d],
            device_id=near[d],
            device_id_type=MESH,
        )

    late_land = jnp.concatenate([land_lanes(p) for p in range(early, pairs)], axis=1).astype(F32)
    late_rows = jnp.concatenate([arrived[p] for p in range(early, pairs)], axis=0)
    for d in (2, 0):
        wanted = index_col[pl.ds(d * border_rows, 2 * border_rows), :]
        hot = jnp.concatenate(
            [
                jnp.where(wanted == late_land[:, 128 * k : 128 * (k + 1)], 1.0, 0.0).astype(BF16)
                for k in range(late_land.shape[1] // 128)
            ],
            axis=1,
        )
        value = get_rows(halo_part, d * border_rows, 2 * border_rows) + jnp.dot(
            hot, late_rows, preferred_element_type=F32
        )
        for q in range(2):
            halo_send[d + q] = value[q * border_rows : (q + 1) * border_rows].astype(BF16)
            halo_copy(d + q).start()

    joined = landed(pairs - 1).astype(BF16)
    rows_bf[...] = joined
    put_rows(rows, 0, cells, joined.astype(F32))

    taps = [dw_ref[q] for q in range(9)]
    gain = gain_ref[...]

    def mix(above, here, below):
        left, mid, right = (
            taps[c] * above + taps[3 + c] * here + taps[6 + c] * below for c in range(3)
        )
        return mid + pltpu.roll(left, 1, 0) + pltpu.roll(right, GRID_W - 1, 0)

    def grid_row(i):
        return get_rows(rows, i * GRID_W, GRID_W)

    def near_row(first):
        return jnp.concatenate(
            [rows_all[pl.ds(margin + 2 * first + h, GRID_W, stride=2), :] for h in range(2)], axis=1
        )

    band = 8
    bands = height // band

    def interior(b, carry):
        for q in range(band):
            i = b * band + q
            mixed = None
            for r in range(3):
                line = jnp.clip(i + r - 1, 0, height - 1) * GRID_W
                for c in range(3):
                    term = taps[3 * r + c] * near_row(line + c - 1)
                    mixed = term if mixed is None else mixed + term
            part = pl.ds(pl.multiple_of(i * GRID_W, GRID_W), GRID_W)
            normed[part, :] = norm(mixed, gain).astype(BF16)
        return carry

    lax.fori_loop(0, bands, interior, 0)

    for copy in small[9:]:
        copy.wait()
    down = (0.5 * down_ref[0].astype(F32)).astype(BF16)

    def mlp(value):
        before = jnp.dot(value, up_ref[0], preferred_element_type=F32) + bias_ref[...]
        return jnp.dot(twice_gelu(before).astype(BF16), down, preferred_element_type=F32)

    def level(first, size):
        part = pl.ds(first, size)
        out[part, :] = (rows_bf[part, :].astype(F32) + mlp(normed[part, :])).astype(BF16)

    def store(k, first, size):
        part = pl.ds(first, size)
        return pltpu.make_async_copy(out.at[part], out_hbm.at[0, part], store_sem.at[k])

    outer = ((1, 0), (2, 1), (3, GRID_W - 2), (4, GRID_W - 1))

    for q, col in outer:
        for h in range(2):
            column = rows[pl.ds(2 * col + h, height, stride=2 * GRID_W), :]
            columns[q, pl.ds(1, height), pl.ds(h * half, half)] = column
    for d in range(4):
        halo_copy(d).wait_recv()

    border[...] = (halo_recv[0].astype(F32) + halo_recv[1].astype(F32)) + (
        halo_recv[2].astype(F32) + halo_recv[3].astype(F32)
    )
    wide = GRID_W + 2
    for q, col in outer:
        columns[q, pl.ds(0, 1), :] = border[pl.ds(1 + col, 1), :]
        columns[q, pl.ds(height + 1, 1), :] = border[pl.ds(wide + 1 + col, 1), :]
    for q, corner, side in ((0, 0, 2 * wide), (5, wide - 1, 2 * wide + height)):
        columns[q, pl.ds(0, 1), :] = border[pl.ds(corner, 1), :]
        columns[q, pl.ds(1, height), :] = border[pl.ds(side, height), :]
        columns[q, pl.ds(height + 1, 1), :] = border[pl.ds(wide + corner, 1), :]
    mixed = [
        mix(border[pl.ds(1, GRID_W), :], grid_row(0), grid_row(1)),
        mix(grid_row(height - 2), grid_row(height - 1), border[pl.ds(wide + 1, GRID_W), :]),
    ]
    for first in (0, 3):
        total = None
        for r in range(3):
            for c in range(3):
                term = taps[3 * r + c] * columns[first + c, pl.ds(r, height), :]
                total = term if total is None else total + term
        mixed.append(total)
    edges = norm(jnp.concatenate(mixed, axis=0), gain)
    line = lax.broadcasted_iota(jnp.int32, (TILE, channels), 0)

    def merge(ref, i, left, right):
        for fresh, first, at in ((left, 0, 0), (right, GRID_W - TILE, TILE - 1)):
            box = pl.ds(i * GRID_W + first, TILE)
            fixed = jnp.where(line == at, fresh, ref[box, :].astype(F32))
            ref[box, :] = fixed.astype(BF16)

    lefts, rights = 2 * GRID_W, 2 * GRID_W + height
    normed[pl.ds(cells - GRID_W, GRID_W), :] = edges[GRID_W : 2 * GRID_W].astype(BF16)
    normed[pl.ds(0, GRID_W), :] = edges[:GRID_W].astype(BF16)
    for i in range(height):
        merge(normed, i, edges[lefts + i : lefts + i + 1], edges[rights + i : rights + i + 1])
    block = 1024
    stores = []
    for first in range(0, cells, block):
        level(first, block)
        stores.append(store(len(stores), first, block))
        stores[-1].start()

    for n in range(tiles):
        cross_copy(n).wait_send()
    for n in range(1, tiles):
        pass_copy(n).wait_send()
    for d in range(4):
        halo_copy(d).wait_send()
    for copy in stores:
        copy.wait()


def twice_gelu(before):
    inner = before * (0.7978845608028654 + 0.035677408136300125 * (before * before))
    return before + before * jnp.tanh(inner)


def body(
    state,
    cycle_source,
    halo_rows,
    halo_count,
    couple_rows,
    couple_count,
    couple_land,
    couple_weight,
    dw_weight,
    norm_gain,
    up_weight,
    up_bias,
    down_weight,
):
    _, cells, channels = state.shape
    tiles, faces = lax.axis_size("tile"), lax.axis_size("face")
    cycle_len = cycle_source.shape[1]
    border_rows = -(-cycle_len // TILE) * TILE
    index_lanes = -(-cycle_len // 128) * 128
    slots = couple_rows.shape[2]
    height = cells // GRID_W
    hbm = pl.BlockSpec(memory_space=pl.ANY)
    dma = pltpu.SemaphoreType.DMA
    vmem = pltpu.VMEM
    return pl.pallas_call(
        functools.partial(couple_kernel, tiles, faces, cycle_len),
        name="couple_and_mix",
        out_shape=jax.ShapeDtypeStruct((1, cells, channels), BF16),
        in_specs=[hbm] * 13,
        out_specs=hbm,
        scratch_shapes=[
            vmem((1, cycle_len), jnp.int32),
            vmem(halo_rows.shape, jnp.int32),
            pltpu.SMEM((1, 4), jnp.int32),
            pltpu.SMEM(couple_rows.shape, jnp.int32),
            pltpu.SMEM((1, tiles), jnp.int32),
            vmem(couple_land.shape, jnp.int32),
            vmem(couple_weight.shape, BF16),
            vmem((9, 1, channels), F32),
            vmem((1, channels), F32),
            vmem(up_weight.shape, BF16),
            vmem(up_bias.shape, F32),
            vmem(down_weight.shape, BF16),
            vmem((cells, channels), BF16),
            vmem((2 * cells + 288, channels // 2), F32),
            vmem((2 * slots + 8, channels // 2), F32),
            vmem((tiles * slots, channels), BF16),
            vmem((tiles * slots, channels), BF16),
            vmem((tiles * slots, channels), BF16),
            vmem((tiles // 2, 2 * slots, channels), BF16),
            vmem((4, 1, cycle_len), jnp.int32),
            vmem((8, index_lanes), jnp.int32),
            pltpu.SMEM((8, index_lanes), jnp.int32),
            vmem((4 * border_rows, 128), F32),
            vmem((4 * 2 * border_rows + 8, channels // 2), F32),
            vmem((4, border_rows, channels), BF16),
            vmem((4, border_rows, channels), BF16),
            vmem((border_rows, channels), F32),
            vmem((6, height + 8, channels), F32),
            vmem((cells, channels), BF16),
            vmem((cells, channels), BF16),
            dma((4,)),
            dma((12,)),
            dma,
            dma((6,)),
            dma((tiles,)),
            dma((tiles,)),
            dma((tiles,)),
            dma((tiles,)),
            dma((4,)),
            dma((4,)),
            dma((4,)),
            dma((4,)),
        ],
        compiler_params=pltpu.CompilerParams(
            collective_id=0, has_side_effects=True, vmem_limit_bytes=64 << 20
        ),
    )(
        state,
        cycle_source,
        halo_rows,
        halo_count.reshape(1, 4),
        couple_rows,
        couple_count.reshape(1, tiles),
        couple_land,
        couple_weight,
        jnp.transpose(dw_weight, (1, 0, 2)),
        norm_gain,
        up_weight,
        up_bias,
        down_weight,
    )


def solution(mesh):
    in_specs = (
        P("comp", ("face", "tile"), None),
        P("comp", ("face", "tile")),
        P("comp", None, ("face", "tile")),
        P("comp", None, ("face", "tile")),
        P("comp", None, ("face", "tile")),
        P("comp", None, ("face", "tile")),
        P("comp", None, ("face", "tile")),
        P("comp", None, None),
        P("comp", None, None),
        P("comp", None),
        P("comp", None, None),
        P("comp", None),
        P("comp", None, None),
    )
    out_specs = P("comp", ("face", "tile"), None)
    return jax.shard_map(body, mesh=mesh, in_specs=in_specs, out_specs=out_specs, check_vma=False)
```
